512 devices in a mesh: seq: 64 (over z, y), vocab: 8 (over x, core).
Axes of the slice: x: 4, y: 4, z: 16, core: 2. Of those that a mesh axis runs over, the one named last changes fastest.
Arguments:
- queries: bfloat16 [512, 8192], P('seq'), may hold values from -32 to 32
- cached_keys: bfloat16 [32768, 1024], P(('seq', 'vocab')), may hold values from -12 to 12
- cached_values: bfloat16 [32768, 1024], P(('seq', 'vocab')), may hold values from -6 to 6
- out_weight: bfloat16 [8192, 5120], P('seq', 'vocab'), may hold values from -0.25 to 0.25
- residual: bfloat16 [512, 5120], P('seq', 'vocab'), may hold values from -64 to 64
- norm_gain: bfloat16 [5120], replicated, may hold values from 0.5 to 1.5
- head_weight: bfloat16 [151552, 5120], P(('seq', 'vocab')), may hold values from -1 to 1
- targets: int32 [512], replicated, may hold values from 0 to 151551
- span_offset: int32 [1], replicated, may hold values from 0 to 32256
Outputs:
- logprob: float32 [512], P('seq')
The draws below stay inside these ranges and needn't reach their ends.
All inputs are finite; a program needn't handle non-finite values.
Results may differ from the reference program's by a relative error of at most 0.0085.
Values may be sent and summed in bfloat16 or wider, within the bound.
A program may use at most 64 MiB of HBM per device.

```python
import math
import jax
import jax.numpy as jnp
from jax import lax

D = 5120
HEADS = 64
KV_HEADS = 8
HEAD_DIM = 128
TOKENS = 512
POSITIONS = 32768
VOCAB = 151552


def draw_queries(key, part):
    key = jax.random.fold_in(key, 3)
    noise_key = jax.random.fold_in(key, 0)
    noise = jax.random.truncated_normal(noise_key, -6.0, 6.0, (TOKENS, HEADS * HEAD_DIM), jnp.float32)
    return (2.0 * noise).astype(jnp.bfloat16)


def draw_cached_keys(key, part):
    key = jax.random.fold_in(key, 4)
    noise_key = jax.random.fold_in(key, 0)
    noise = jax.random.truncated_normal(noise_key, -6.0, 6.0, (POSITIONS, KV_HEADS * HEAD_DIM), jnp.float32)
    return noise.astype(jnp.bfloat16)


def draw_residual(key, part):
    key = jax.random.fold_in(key, 1)
    noise_key = jax.random.fold_in(key, 0)
    column = jnp.arange(D, dtype=jnp.float32) / (D - 1)
    noise = jax.random.truncated_normal(noise_key, -6.0, 6.0, (TOKENS, D), jnp.float32)
    return (noise * (0.3 * 4.0 ** column)[None, :]).astype(jnp.bfloat16)


def draw_head_weight(key, part):
    key = jax.random.fold_in(key, 2)
    row_share = (jnp.arange(VOCAB, dtype=jnp.float32) / (VOCAB - 1))[:, None]
    noise = jax.random.truncated_normal(key, -6.0, 6.0, (VOCAB, D), jnp.float32)
    return (noise * (3.0 * (3.35 / 3.0) ** row_share) / math.sqrt(D)).astype(jnp.bfloat16)


def plant(result, own_key, smallest, high):
    shape = result.shape
    place = [jax.random.randint(jax.random.fold_in(own_key, axis), (), 0, shape[axis]) for axis in range(len(shape))]
    result = result.at[tuple(place)].set(smallest)
    longest = shape.index(max(shape))
    place[longest] = (place[longest] + 1) % shape[longest]
    return result.at[tuple(place)].set(high)


def levels(rng, extent, pieces, least, top_value):
    loudness, own = 1.0, jax.random.fold_in(rng, 6)
    for axis_at, shards_of in pieces:
        steps = jnp.exp(jax.random.uniform(jax.random.fold_in(own, axis_at), (shards_of,), jnp.float32, least / len(pieces), top_value / len(pieces)))
        loudness = loudness * jnp.repeat(steps, extent[axis_at] // shards_of).reshape([-1 if axis == axis_at else 1 for axis in range(len(extent))])
    return loudness


def gaussian(key, extent, scale, limit, cuts=(), kind=jnp.bfloat16):
    entries = jax.random.normal(key, extent, jnp.float32) * scale
    if len(cuts) > 0:
        entries = levels(key, extent, cuts, -0.22, 0.18) * entries
    return jnp.clip(entries, min=-limit, max=limit).astype(kind)


def setup_inputs(seed: int = 0) -> dict:
    key_list = jax.random.split(jax.random.key(seed), 10)
    queries = draw_queries(jax.random.fold_in(key_list[9], 71), 0)
    cached_keys = draw_cached_keys(jax.random.fold_in(key_list[9], 71), 0)
    cached_values = gaussian(key_list[2], (POSITIONS, KV_HEADS * HEAD_DIM), 1.0, 6.0, ((0, 512),))
    out_weight = gaussian(key_list[3], (HEADS * HEAD_DIM, D), (HEADS * HEAD_DIM // 16) ** -0.5, 0.25, ((0, 64), (1, 8)))
    residual = draw_residual(jax.random.fold_in(key_list[9], 71), 0)
    norm_gain = jnp.clip(1.0 + 0.1 * jax.random.normal(key_list[5], (D,), jnp.float32), 0.5, 1.5).astype(jnp.bfloat16)
    head_weight = draw_head_weight(jax.random.fold_in(key_list[9], 71), 0)
    targets = plant(jax.random.randint(key_list[7], (TOKENS,), 0, VOCAB), jax.random.fold_in(key_list[7], 1), 0, VOCAB - 1).astype(jnp.int32)
    span_offset = jax.random.randint(key_list[8], (1,), 0, POSITIONS - TOKENS + 1).astype(jnp.int32)
    return dict(queries=queries, cached_keys=cached_keys, cached_values=cached_values, out_weight=out_weight, residual=residual, norm_gain=norm_gain, head_weight=head_weight, targets=targets, span_offset=span_offset)


def reference(queries, cached_keys, cached_values, out_weight, residual, norm_gain, head_weight, targets, span_offset):
    group_size = HEADS // KV_HEADS
    query_heads = queries.reshape(TOKENS, HEADS, HEAD_DIM)
    key_heads = cached_keys.reshape(POSITIONS, KV_HEADS, HEAD_DIM)
    value_heads = cached_values.reshape(POSITIONS, KV_HEADS, HEAD_DIM)
    query_pos = span_offset[0] + jnp.arange(TOKENS, dtype=jnp.int32)
    visible = jnp.arange(POSITIONS, dtype=jnp.int32)[None, :] <= query_pos[:, None]
    inv_scale = 1.0 / math.sqrt(HEAD_DIM)

    def one_head(head_index):
        query_one = lax.dynamic_index_in_dim(query_heads, head_index, 1, keepdims=False)
        key_one = lax.dynamic_index_in_dim(key_heads, head_index // group_size, 1, keepdims=False)
        value_one = lax.dynamic_index_in_dim(value_heads, head_index // group_size, 1, keepdims=False)
        scores = lax.dot_general(query_one, key_one, (((1,), (1,)), ((), ())), preferred_element_type=jnp.float32) * inv_scale
        scores = jnp.where(visible, scores, -jnp.inf)
        row_top = lax.optimization_barrier(jnp.max(scores, axis=1, keepdims=True))
        weights = jnp.exp(scores - row_top)
        weight_sum = lax.optimization_barrier(jnp.sum(weights, axis=1, keepdims=True))
        mixed_values = jnp.dot(weights.astype(jnp.bfloat16), value_one, preferred_element_type=jnp.float32)
        return (mixed_values / weight_sum).astype(jnp.bfloat16)
    attended = lax.map(one_head, jnp.arange(HEADS, dtype=jnp.int32))
    projected = jnp.einsum('hqd,hde->qe', attended.astype(jnp.float32), out_weight.reshape(HEADS, HEAD_DIM, D).astype(jnp.float32))
    hidden_state = residual.astype(jnp.float32) + projected
    mean_square = lax.optimization_barrier(jnp.mean(hidden_state * hidden_state, axis=1, keepdims=True))
    normed = (hidden_state * lax.rsqrt(mean_square + 1e-06) * norm_gain.astype(jnp.float32)).astype(jnp.bfloat16)
    logits = lax.dot_general(normed, head_weight, (((1,), (1,)), ((), ())), preferred_element_type=jnp.float32)
    row_top = lax.optimization_barrier(jnp.max(logits, axis=1))
    exp_total = lax.optimization_barrier(jnp.sum(jnp.exp(logits - row_top[:, None]), axis=1))
    picked = jnp.take_along_axis(logits, targets[:, None], axis=1)[:, 0]
    return picked - row_top - jnp.log(exp_total)
```

```python
import math

import jax
import jax.numpy as jnp
from jax import lax
from jax.experimental import pallas as pl
from jax.experimental.pallas import tpu as pltpu
from jax.sharding import PartitionSpec as P

MESH = pl.DeviceIdType.MESH
HEAD_DIM = 128
NZ, NY, NX, NC = 16, 4, 4, 2
NV = NX * NC
WIDTH = 5120
COLS = WIDTH // NV
ROWS = 296
FLOOR = 1e-06
LOW = -1e30
F32 = jnp.float32
BF16 = jnp.bfloat16


def split3(x):
    hi = x.astype(BF16).astype(F32)
    rest = x - hi
    mid = rest.astype(BF16).astype(F32)
    lo = (rest - mid).astype(BF16).astype(F32)
    return hi, mid, lo


def nt(a, b, precision=None):
    return lax.dot_general(
        a, b, (((1,), (1,)), ((), ())), preferred_element_type=F32, precision=precision
    )


def kernel(
    span_ref,
    q_ref,
    k_ref,
    v_ref,
    w_ref,
    res_ref,
    gain_ref,
    ginv_ref,
    head_ref,
    tgt_ref,
    out_ref,
    q1src,
    q1buf,
    qall,
    kvbuf,
    vt,
    sbuf,
    osend,
    obuf,
    psrc,
    pbuf,
    att,
    abuf,
    wbuf,
    prsend,
    prbuf,
    hsend,
    hall,
    whead,
    logit,
    stsrc,
    stbuf,
    stplane,
    stz,
    kv_s,
    kv_r,
    q1_s,
    q1_r,
    kf_s,
    kf_r,
    qa_s,
    qa_r,
    o_s,
    o_r,
    p_s,
    p_r,
    a_s,
    a_r,
    w_s,
    w_r,
    pr_s,
    pr_r,
    h_s,
    h_r,
    h1_s,
    h1_r,
    h2_s,
    h2_r,
    hw_s,
    hw_r,
    t1_s,
    t1_r,
    t2_s,
    t2_r,
    loc,
):
    s = lax.axis_index("seq")
    v = lax.axis_index("vocab")
    z, y, x, c = s // NY, s % NY, v // NC, v % NC
    g, par = z // 2, z % 2

    def dev(zz, yy, xx, cc):
        return (zz * NY + yy, xx * NC + cc)

    def wrap(a, n):
        return lax.rem(a + n, n)

    def push(src, dst, ss, rs, to):
        cp = pltpu.make_async_remote_copy(
            src_ref=src, dst_ref=dst, send_sem=ss, recv_sem=rs, device_id=to, device_id_type=MESH
        )
        cp.start()

    def got(ref, sem):
        pltpu.make_async_copy(ref, ref, sem).wait()

    own_head = pltpu.make_async_copy(head_ref, whead.at[0], loc.at[0])
    own_head.start()
    own_w = pltpu.make_async_copy(w_ref, wbuf.at[y], loc.at[1])
    own_w.start()
    own_k = pltpu.make_async_copy(
        k_ref.at[:, pl.ds(pl.multiple_of(g * 128, 128), 128)], kvbuf.at[y, g, 0], loc.at[2]
    )
    own_k.start()
    own_v = pltpu.make_async_copy(
        v_ref.at[:, pl.ds(pl.multiple_of(g * 128, 128), 128)], kvbuf.at[y, g, 1], loc.at[3]
    )
    own_v.start()

    barrier = pltpu.get_barrier_semaphore()

    def greet(zz, yy, xx, cc):
        pl.semaphore_signal(barrier, inc=1, device_id=dev(zz, yy, xx, cc), device_id_type=MESH)

    @pl.loop(1, NZ)
    def _(d):
        greet(wrap(z + d, NZ), y, x, c)
        greet(wrap(z + d, NZ), y, x, 1 - c)

    greet(z, y, x, 1 - c)
    for dx in range(1, NX):
        greet(z, y, wrap(x + dx, NX), 1 - c)
    for dy in range(NY):
        for dx in range(NX):
            if (dy, dx) != (0, 0):
                greet(z, wrap(y + dy, NY), wrap(x + dx, NX), c)

    q_f = q_ref[...].astype(F32)
    pick_row = lax.broadcasted_iota(jnp.int32, (8, 128), 0) == v
    for h in range(64):
        row = jnp.sum(
            jnp.where(pick_row, q_f[:, h * 128 : (h + 1) * 128], 0.0), axis=0, keepdims=True
        )
        q1src[h // 8, h % 8 : h % 8 + 1, :] = row

    pl.semaphore_wait(barrier, 2 * (NZ - 1) + 1 + (NX - 1) + NY * NX - 1)

    @pl.loop(1, NZ)
    def _(d):
        to = wrap(z + d, NZ)
        push(q1src.at[to // 2], q1buf.at[z], q1_s.at[d], q1_r.at[z], dev(to, y, x, c))

    @pl.loop(1, 8)
    def _(d):
        head = wrap(g + d, 8)
        to = dev(2 * head + par, y, x, c)
        cols = pl.ds(pl.multiple_of(head * 128, 128), 128)
        push(k_ref.at[:, cols], kvbuf.at[y, g, 0], kv_s.at[d, 0], kv_r.at[g, 0], to)
        push(v_ref.at[:, cols], kvbuf.at[y, g, 1], kv_s.at[d, 1], kv_r.at[g, 1], to)

    for d in range(1, NY):
        push(w_ref, wbuf.at[y], w_s.at[d], w_r.at[y], dev(z, wrap(y + d, NY), x, c))
    push(head_ref, whead.at[1], hw_s.at[0], hw_r.at[0], dev(z, y, x, 1 - c))

    q1buf[z] = q1src[g]

    @pl.loop(1, NZ)
    def _(d):
        frm = wrap(z - d + NZ, NZ)
        got(q1buf.at[frm], q1_r.at[frm])

    ri = lax.broadcasted_iota(jnp.int32, (128, 128), 0)
    ci = lax.broadcasted_iota(jnp.int32, (128, 128), 1)
    to_heads = (ci == (ri % 16) * 8 + ri // 16).astype(BF16)
    q_rows = q1buf[...].reshape(128, 128).astype(BF16)
    qall[v] = jnp.dot(to_heads, q_rows, preferred_element_type=F32).astype(BF16)

    @pl.loop(1, NV)
    def _(k):
        o = wrap(v + k, NV)
        push(qall.at[v], qall.at[v], qa_s.at[k], qa_r.at[v], dev(z, y, o // NC, o % NC))

    own_k.wait()
    own_v.wait()

    @pl.loop(0, 8)
    def _(d):
        frm = wrap(g - d + 8, 8)

        @pl.when(d > 0)
        def _():
            got(kvbuf.at[y, frm, 0], kv_r.at[frm, 0])
            got(kvbuf.at[y, frm, 1], kv_r.at[frm, 1])

        for e in range(1, NY):
            push(
                kvbuf.at[y, frm],
                kvbuf.at[y, frm],
                kf_s.at[frm, e],
                kf_r.at[y, frm],
                dev(z, wrap(y + e, NY), x, c),
            )

    for e in range(1, NY):
        frm_y = wrap(y - e + NY, NY)

        @pl.loop(0, 8)
        def _(j):
            got(kvbuf.at[frm_y, j], kf_r.at[frm_y, j])

    for yy in range(NY):
        vt[:, yy * 512 : (yy + 1) * 512] = kvbuf[yy, :, 1].reshape(512, 128).T

    span = span_ref[0]
    scale = 1.0 / math.sqrt(HEAD_DIM)
    rho = lax.broadcasted_iota(jnp.int32, (512, 128), 0)
    lane = lax.broadcasted_iota(jnp.int32, (512, 128), 1)
    pos = (rho // 64) * 4096 + rho % 64 + ((4 * par) * 8 + v) * 64
    tok = 8 * (4 * (lane % 16) + y) + span

    @pl.loop(1, NV + 1)
    def _(k):
        o = wrap(v + k, NV)

        @pl.when(k < NV)
        def _():
            got(qall.at[o], qa_r.at[o])

        q_blk = qall[o]
        top = jnp.full((1, 128), LOW, F32)
        for yy in range(NY):
            scores = nt(kvbuf[yy, :, 0].reshape(512, 128), q_blk) * scale
            live = pos + yy * 512 <= tok + o
            scores = jnp.where(live, scores, LOW)
            sbuf[yy] = scores
            top = jnp.maximum(top, jnp.max(scores, axis=0, keepdims=True))
        total = jnp.zeros((1, 128), F32)
        acc = jnp.zeros((128, 128), F32)
        for yy in range(NY):
            live = pos + yy * 512 <= tok + o
            wts = jnp.where(live, jnp.exp(sbuf[yy] - top), 0.0)
            total = total + jnp.sum(wts, axis=0, keepdims=True)
            acc = acc + jnp.dot(
                vt[:, yy * 512 : (yy + 1) * 512], wts.astype(BF16), preferred_element_type=F32
            )
        stats = jnp.concatenate(
            list(split3(top)) + list(split3(total)) + [jnp.zeros((10, 128), F32)], axis=0
        )
        osend[o, 0:128, :] = acc.astype(BF16)
        osend[o, 128:144, :] = stats.astype(BF16)

        @pl.when(k < NV)
        def _():
            push(osend.at[o], obuf.at[v], o_s.at[k], o_r.at[v], dev(z, y, o // NC, o % NC))

    def unpack(block):
        b = block.astype(F32)
        return (
            b[128:129] + b[129:130] + b[130:131],
            b[131:132] + b[132:133] + b[133:134],
            b[0:128],
        )

    def blend(one, two):
        m1, l1, a1 = one
        m2, l2, a2 = two
        m = jnp.maximum(m1, m2)
        f1, f2 = jnp.exp(m1 - m), jnp.exp(m2 - m)
        return m, l1 * f1 + l2 * f2, a1 * f1 + a2 * f2

    def take_share(k, state):
        frm = wrap(v - k + NV, NV)
        got(obuf.at[frm], o_r.at[frm])
        return blend(state, unpack(obuf[frm]))

    state = lax.fori_loop(1, NV, take_share, unpack(osend[v]))

    m_own, l_own, a_own = state
    stats = jnp.concatenate(
        list(split3(m_own)) + list(split3(l_own)) + [jnp.zeros((10, 128), F32)], axis=0
    )
    psrc[0:128, :] = a_own.astype(BF16)
    psrc[128:144, :] = stats.astype(BF16)
    push(psrc, pbuf, p_s.at[0], p_r.at[0], dev(z + 1 - 2 * par, y, x, c))
    got(pbuf, p_r.at[0])
    _, l_all, a_all = blend(state, unpack(pbuf[...]))
    att[...] = (a_all / l_all).T.astype(BF16)

    mine = att.at[pl.ds(pl.multiple_of(par * 64, 64), 64)]

    @pl.loop(1, NV)
    def _(k):
        o = wrap(v + k, NV)
        push(mine, abuf.at[v], a_s.at[k], a_r.at[v], dev(z, y, o // NC, o % NC))

    abuf[v] = att[pl.ds(pl.multiple_of(par * 64, 64), 64), :]
    own_w.wait()
    for d in range(1, NY):
        frm_y = wrap(y - d + NY, NY)
        got(wbuf.at[frm_y], w_r.at[frm_y])

    @pl.loop(1, NV)
    def _(k):
        frm = wrap(v - k + NV, NV)
        got(abuf.at[frm], a_r.at[frm])

    proj = jnp.zeros((128, COLS), F32)
    for h in range(4):
        rows = abuf[:, h * 16 : (h + 1) * 16, :].reshape(128, 128)
        proj = proj + jnp.dot(rows, wbuf[h], preferred_element_type=F32)
    to_planes = (ci == (ri % 8) * 16 + ri // 8).astype(BF16)
    by_plane = jnp.dot(to_planes, proj.astype(BF16), preferred_element_type=F32)
    prsend[...] = by_plane.reshape(NZ, 8, COLS).astype(BF16)

    @pl.loop(1, NZ)
    def _(d):
        to = wrap(z + d, NZ)
        push(prsend.at[to], prbuf.at[z], pr_s.at[d], pr_r.at[z], dev(to, y, x, c))

    def add_share(d, total):
        frm = wrap(z - d + NZ, NZ)
        got(prbuf.at[frm], pr_r.at[frm])
        return total + prbuf[frm].astype(F32)

    hidden = lax.fori_loop(
        1, NZ, add_share, res_ref[...].astype(F32) + prsend[z].astype(F32)
    )
    hsend[...] = (hidden * gain_ref[v]).astype(BF16)

    half, low = z // 8, z % 8

    @pl.loop(1, NZ)
    def _(d):
        to = wrap(z + d, NZ)
        push(hsend, hall.at[y, x, low, c], h_s.at[d], h_r.at[low, c], dev(to, y, x, half))

    @pl.when(c == half)
    def _():
        keep = pltpu.make_async_copy(hsend, hall.at[y, x, low, c], h_r.at[low, c])
        keep.start()

    @pl.when(c != half)
    def _():
        push(hsend, hall.at[y, x, low, c], h_s.at[0], h_r.at[low, c], dev(z, y, x, half))

    @pl.loop(0, 8)
    def _(j):
        for cc in range(NC):
            got(hall.at[y, x, j, cc], h_r.at[j, cc])

    for d in range(1, 4):
        first = hall.at[y, x, pl.ds(0, 4)]
        push(first, first, h1_s.at[0, d], h1_r.at[0, x], dev(z, y, wrap(x + d, NX), c))
        second = hall.at[y, x, pl.ds(4, 4)]
        push(second, second, h1_s.at[1, d], h1_r.at[1, y], dev(z, wrap(y + d, NY), x, c))

    for e in range(4):
        xx, yy = wrap(x + e, NX), wrap(y + e, NY)
        first = hall.at[y, xx, pl.ds(0, 4)]
        second = hall.at[yy, x, pl.ds(4, 4)]
        if e > 0:
            got(first, h1_r.at[0, xx])
            got(second, h1_r.at[1, yy])
        for d in range(1, 4):
            push(first, first, h2_s.at[0, e, d], h2_r.at[0, y, xx], dev(z, wrap(y + d, NY), x, c))
            push(second, second, h2_s.at[1, e, d], h2_r.at[1, x, yy], dev(z, y, wrap(x + d, NX), c))

    own_head.wait()
    got(whead.at[1], hw_r.at[0])
    for d in range(1, 4):
        frm_y, frm_x = wrap(y + d, NY), wrap(x + d, NX)
        for e in range(4):
            got(hall.at[frm_y, e, pl.ds(0, 4)], h2_r.at[0, frm_y, e])
            got(hall.at[e, frm_x, pl.ds(4, 4)], h2_r.at[1, frm_x, e])

    logit[...] = jnp.zeros_like(logit)

    def head_step(n, squares):
        hid = hall[:, n // 2, :, n % 2].astype(F32).reshape(256, COLS)
        squares = squares + nt(ginv_ref[n], hid * hid, lax.Precision.HIGHEST)
        hid16 = hid.astype(BF16)
        cols = pl.ds(pl.multiple_of(n * COLS, 128), COLS)
        for p in range(2):
            logit[p] += nt(whead[p, :, cols], hid16)
        return squares

    squares = lax.fori_loop(0, NV, head_step, jnp.zeros((8, 256), F32))
    row_scale = lax.rsqrt(squares[0:1] / WIDTH + FLOOR)
    targets = tgt_ref[c]
    row_id = lax.broadcasted_iota(jnp.int32, (ROWS, 256), 0)
    tops, parts, picks = [], [], []
    for p in range(2):
        block = s * NV + (v if p == 0 else v + 1 - 2 * c)
        lg = logit[p] * row_scale
        logit[p] = lg
        picks.append(
            jnp.sum(jnp.where(row_id == targets - block * ROWS, lg, 0.0), axis=0, keepdims=True)
        )
        tops.append(jnp.max(lg, axis=0, keepdims=True))
    top = jnp.maximum(tops[0], tops[1])
    for p in range(2):
        parts.append(jnp.sum(jnp.exp(logit[p] - top), axis=0, keepdims=True))
    stsrc[...] = jnp.concatenate(
        [top, parts[0] + parts[1], picks[0] + picks[1], jnp.zeros((5, 256), F32)], axis=0
    )

    def join(one, two):
        m = jnp.maximum(one[0:1], two[0:1])
        t = one[1:2] * jnp.exp(one[0:1] - m) + two[1:2] * jnp.exp(two[0:1] - m)
        return jnp.concatenate([m, t, one[2:3] + two[2:3], one[3:8]], axis=0)

    q = y * NX + x

    @pl.loop(1, 16)
    def _(k):
        o = wrap(q + k, 16)
        push(stsrc, stbuf.at[q], t1_s.at[k], t1_r.at[q], dev(z, o // NX, o % NX, c))

    def join_plane(k, state):
        frm = wrap(q - k + 16, 16)
        got(stbuf.at[frm], t1_r.at[frm])
        return join(state, stbuf[frm])

    plane = lax.fori_loop(1, 16, join_plane, stsrc[...])
    stplane[0] = plane[:, 0:128]
    stplane[1] = plane[:, 128:256]

    side = y // 2

    @pl.loop(0, 8)
    def _(j):
        to = 8 * c + j

        @pl.when(to != z)
        def _():
            for cc in range(NC):
                push(stplane.at[side], stz.at[z], t2_s.at[j, cc], t2_r.at[z], dev(to, y, x, cc))

        @pl.when(to == z)
        def _():
            push(stplane.at[side], stz.at[z], t2_s.at[j, 0], t2_r.at[z], dev(z, y, x, 1 - c))
            keep = pltpu.make_async_copy(stplane.at[side], stz.at[z], t2_r.at[z])
            keep.start()

    @pl.loop(0, NZ)
    def _(j):
        got(stz.at[j], t2_r.at[j])

    final = stz[0]
    for j in range(1, NZ):
        final = join(final, stz[j])
    logprob = final[2:3] - final[0:1] - jnp.log(final[1:2])
    shift = lax.rem(128 - ((y % 2) * 64 + (z % 8) * 8), 128)
    out_ref[...] = pltpu.roll(jnp.broadcast_to(logprob, (8, 128)), shift, 1)

    @pl.loop(1, NZ)
    def _(d):
        got(q1src.at[0], q1_s.at[d])
        got(prsend.at[0], pr_s.at[d])
        got(hsend, h_s.at[d])

    @pl.when(c != half)
    def _():
        got(hsend, h_s.at[0])

    @pl.loop(1, 8)
    def _(d):
        got(kvbuf.at[0, 0, 0], kv_s.at[d, 0])
        got(kvbuf.at[0, 0, 1], kv_s.at[d, 1])
        got(qall.at[0], qa_s.at[d])
        got(osend.at[0], o_s.at[d])
        got(abuf.at[0], a_s.at[d])

    for e in range(1, NY):
        got(wbuf.at[0], w_s.at[e])

        @pl.loop(0, 8)
        def _(j):
            got(kvbuf.at[0, 0], kf_s.at[j, e])

    got(whead.at[1], hw_s.at[0])
    got(psrc, p_s.at[0])
    for d in range(1, 4):
        for i in range(2):
            got(hall.at[0, 0, pl.ds(0, 4)], h1_s.at[i, d])
            for e in range(4):
                got(hall.at[0, 0, pl.ds(0, 4)], h2_s.at[i, e, d])

    @pl.loop(1, 16)
    def _(k):
        got(stsrc, t1_s.at[k])

    @pl.loop(0, 8)
    def _(j):
        got(stplane.at[0], t2_s.at[j, 0])

        @pl.when(8 * c + j != z)
        def _():
            got(stplane.at[0], t2_s.at[j, 1])


def body(
    queries,
    cached_keys,
    cached_values,
    out_weight,
    residual,
    norm_gain,
    head_weight,
    targets,
    span_offset,
):
    gain = norm_gain.astype(F32).reshape(NV, 1, COLS)
    gain_inv = jnp.broadcast_to(1.0 / (gain * gain), (NV, 8, COLS))
    tgt = targets.reshape(2, 8, NY, 8).transpose(0, 2, 1, 3).reshape(2, 1, 256)
    vm = pl.BlockSpec(memory_space=pltpu.VMEM)
    hbm = pl.BlockSpec(memory_space=pl.ANY)
    dma = pltpu.SemaphoreType.DMA
    out = pl.pallas_call(
        kernel,
        out_shape=jax.ShapeDtypeStruct((8, 128), F32),
        in_specs=[pl.BlockSpec(memory_space=pltpu.SMEM), vm, hbm, hbm, hbm, vm, vm, vm, hbm, vm],
        out_specs=vm,
        scratch_shapes=[
            pltpu.VMEM((8, 8, 128), F32),
            pltpu.VMEM((NZ, 8, 128), F32),
            pltpu.VMEM((NV, 128, 128), BF16),
            pltpu.VMEM((NY, 8, 2, 64, 128), BF16),
            pltpu.VMEM((128, 2048), BF16),
            pltpu.VMEM((NY, 512, 128), F32),
            pltpu.VMEM((NV, 144, 128), BF16),
            pltpu.VMEM((NV, 144, 128), BF16),
            pltpu.VMEM((144, 128), BF16),
            pltpu.VMEM((144, 128), BF16),
            pltpu.VMEM((128, 128), BF16),
            pltpu.VMEM((NV, 64, 128), BF16),
            pltpu.VMEM((NY, 128, COLS), BF16),
            pltpu.VMEM((NZ, 8, COLS), BF16),
            pltpu.VMEM((NZ, 8, COLS), BF16),
            pltpu.VMEM((8, COLS), BF16),
            pltpu.VMEM((NY, NX, 8, NC, 8, COLS), BF16),
            pltpu.VMEM((2, ROWS, WIDTH), BF16),
            pltpu.VMEM((2, ROWS, 256), F32),
            pltpu.VMEM((8, 256), F32),
            pltpu.VMEM((16, 8, 256), F32),
            pltpu.VMEM((2, 8, 128), F32),
            pltpu.VMEM((NZ, 8, 128), F32),
            dma((8, 2)),
            dma((8, 2)),
            dma((NZ,)),
            dma((NZ,)),
            dma((8, NY)),
            dma((NY, 8)),
            dma((NV,)),
            dma((NV,)),
            dma((NV,)),
            dma((NV,)),
            dma((1,)),
            dma((1,)),
            dma((NV,)),
            dma((NV,)),
            dma((NY,)),
            dma((NY,)),
            dma((NZ,)),
            dma((NZ,)),
            dma((NZ,)),
            dma((8, NC)),
            dma((2, 4)),
            dma((2, 4)),
            dma((2, 4, 4)),
            dma((2, 4, 4)),
            dma((1,)),
            dma((1,)),
            dma((16,)),
            dma((16,)),
            dma((8, NC)),
            dma((NZ,)),
            dma((4,)),
        ],
        compiler_params=pltpu.CompilerParams(
            collective_id=0, has_side_effects=True, vmem_limit_bytes=48 * 2**20
        ),
        cost_estimate=pl.CostEstimate(
            flops=3_000_000_000, bytes_accessed=8_000_000, transcendentals=2_500_000
        ),
    )(
        span_offset,
        queries,
        cached_keys,
        cached_values,
        out_weight,
        residual,
        gain,
        gain_inv,
        head_weight,
        tgt,
    )
    return out[0, :8]


def solution(mesh):
    return jax.shard_map(
        body,
        mesh=mesh,
        in_specs=(
            P("seq", None),
            P(("seq", "vocab"), None),
            P(("seq", "vocab"), None),
            P("seq", "vocab"),
            P("seq", "vocab"),
            P(),
            P(("seq", "vocab"), None),
            P(),
            P(),
        ),
        out_specs=P("seq"),
        check_vma=False,
    )
```

```python
import math

import jax
import jax.numpy as jnp
from jax import lax
from jax.experimental import pallas as pl
from jax.experimental.pallas import tpu as pltpu
from jax.sharding import PartitionSpec as P

MESH = pl.DeviceIdType.MESH
HEAD_DIM = 128
NZ, NY, NX, NC = 16, 4, 4, 2
NV = NX * NC
WIDTH = 5120
COLS = WIDTH // NV
ROWS = 296
FLOOR = 1e-06
LOW = -1e30
F32 = jnp.float32
BF16 = jnp.bfloat16


def split3(x):
    hi = x.astype(BF16).astype(F32)
    rest = x - hi
    mid = rest.astype(BF16).astype(F32)
    lo = (rest - mid).astype(BF16).astype(F32)
    return hi, mid, lo


def nt(a, b, precision=None):
    return lax.dot_general(
        a, b, (((1,), (1,)), ((), ())), preferred_element_type=F32, precision=precision
    )


def kernel(
    span_ref,
    q_ref,
    k_ref,
    v_ref,
    w_ref,
    res_ref,
    gain_ref,
    head_ref,
    tgt_ref,
    out_ref,
    span_m,
    q_m,
    res_m,
    gain_m,
    tgt_m,
    gain_n,
    ginv_n,
    tgt_n,
    diff,
    q1src,
    q1buf,
    qall,
    kbuf,
    vbuf,
    wts_m,
    acc_m,
    run_m,
    osend,
    obuf,
    psrc,
    pbuf,
    att,
    abuf,
    wbuf,
    prsend,
    prbuf,
    hsend,
    hall,
    whead,
    logit,
    stsrc,
    stz,
    stred,
    stfin,
    kv_s,
    kv_r,
    kf_s,
    vf_s,
    kf_r,
    vf_r,
    q1_s,
    q1_r,
    qa_s,
    qa_r,
    o_s,
    o_r,
    p_s,
    p_r,
    a_s,
    a_r,
    w_s,
    w_r,
    wf_s,
    pr_s,
    pr_r,
    h_s,
    h_r,
    h1_s,
    h1_r,
    h2_s,
    h2_r,
    hw_s,
    hw_r,
    t1_s,
    t1_r,
    t2_s,
    t2_r,
    loc,
):
    s = lax.axis_index("seq")
    v = lax.axis_index("vocab")
    z, y, x, c = s // NY, s % NY, v // NC, v % NC
    g, par = z // 2, z % 2
    q = y * NX + x

    def dev(zz, yy, xx, cc):
        return (zz * NY + yy, xx * NC + cc)

    def wrap(a, n):
        return lax.rem(a + n, n)

    def flip(a, k):
        swaps = (a, a + 1 - 2 * lax.rem(a, 2), lax.rem(a + 2, 4), 3 - a)
        if isinstance(k, int):
            return swaps[k]
        return jnp.where(
            k < 2, jnp.where(k == 0, swaps[0], swaps[1]), jnp.where(k == 2, swaps[2], swaps[3])
        )

    def push(src, dst, ss, rs, to):
        cp = pltpu.make_async_remote_copy(
            src_ref=src, dst_ref=dst, send_sem=ss, recv_sem=rs, device_id=to, device_id_type=MESH
        )
        cp.start()

    def got(ref, sem):
        pltpu.make_async_copy(ref, ref, sem).wait()

    own_head = pltpu.make_async_copy(head_ref, whead.at[0], loc.at[0])
    own_head.start()
    own_w = pltpu.make_async_copy(w_ref, wbuf.at[par, y], loc.at[1])
    own_w.start()
    own_k = pltpu.make_async_copy(
        k_ref.at[:, pl.ds(pl.multiple_of(g * 128, 128), 128)], kbuf.at[y, 0], loc.at[2]
    )
    own_k.start()
    own_v = pltpu.make_async_copy(
        v_ref.at[:, pl.ds(pl.multiple_of(g * 128, 128), 128)], vbuf.at[y, 0], loc.at[3]
    )
    own_v.start()
    loads = [
        pltpu.make_async_copy(a, b, loc.at[4 + i])
        for i, (a, b) in enumerate(
            (
                (q_ref, q_m),
                (gain_ref, gain_m),
                (tgt_ref, tgt_m),
                (span_ref, span_m),
                (res_ref, res_m),
            )
        )
    ]
    for cp in loads:
        cp.start()

    barrier = pltpu.get_barrier_semaphore()

    def greet(zz, yy, xx, cc):
        pl.semaphore_signal(barrier, inc=1, device_id=dev(zz, yy, xx, cc), device_id_type=MESH)

    @pl.loop(1, NZ)
    def _(d):
        greet(wrap(z + d, NZ), y, x, c)
        greet(wrap(z + d, NZ), y, x, 1 - c)

    greet(z, y, x, 1 - c)
    for k in range(1, 16):
        for cc in range(NC):
            greet(z, flip(y, k // 4), flip(x, k % 4), cc)

    for cp in loads:
        cp.wait()
    q_f = q_m[...].astype(F32)
    pick_row = lax.broadcasted_iota(jnp.int32, (8, 128), 0) == v
    for gg in range(8):
        rows = []
        for h in range(8 * gg, 8 * gg + 8):
            part = jnp.where(pick_row, q_f[:, h * 128 : (h + 1) * 128], 0.0)
            rows.append(jnp.sum(part, axis=0, keepdims=True))
        q1src[gg] = jnp.concatenate(rows, axis=0).astype(BF16)

    pl.semaphore_wait(barrier, 2 * (NZ - 1) + 31)

    @pl.loop(1, NZ)
    def _(d):
        to = wrap(z + d, NZ)
        push(q1src.at[to // 2], q1buf.at[z], q1_s.at[d], q1_r.at[z], dev(to, y, x, c))

    def spread(src, dst, i):
        @pl.loop(1, 8)
        def _(d):
            head = wrap(g + d, 8)
            ahead = 2 * d - par
            up = ahead <= 7
            to = dev(2 * head + jnp.where(up, 0, 1), y, x, c)
            k = jnp.where(up, ahead, 15 - ahead)
            cols = pl.ds(pl.multiple_of(head * 128, 128), 128)
            push(src.at[:, cols], dst.at[y, k], kv_s.at[d, i], kv_r.at[k, i], to)

    spread(k_ref, kbuf, 0)
    spread(v_ref, vbuf, 1)

    for d in range(1, NY):
        push(w_ref, wbuf.at[par, y], w_s.at[d], w_r.at[par, y], dev(z, wrap(y + d, NY), x, c))
    push(head_ref, whead.at[1], hw_s.at[0], hw_r.at[0], dev(z, y, x, 1 - c))

    gains = gain_m[...].astype(F32).reshape(WIDTH // 128, 128)
    for t in range(WIDTH // 128):
        one = gains[t : t + 1]
        lanes = slice((t % 5) * 128, (t % 5 + 1) * 128)
        gain_n[t // 5, :, lanes] = one
        ginv_n[t // 5, :, lanes] = jnp.broadcast_to(1.0 / (one * one), (8, 128))
    tgt4 = tgt_m[...].reshape(4, 128).astype(F32)
    src = lax.broadcasted_iota(jnp.int32, (128, 256), 0)
    dst = lax.broadcasted_iota(jnp.int32, (128, 256), 1)
    plane_of = lax.rem(dst // 32 + z, 8)
    here = src == (plane_of % 4) * 32 + dst % 32
    ordered = jnp.zeros((8, 256), F32)
    for r in range(2):
        row = jnp.where(c == 0, tgt4[r : r + 1], tgt4[2 + r : 3 + r])
        ordered = ordered + jnp.dot(
            jnp.broadcast_to(row, (8, 128)),
            jnp.where(here & (plane_of // 4 == r), 1.0, 0.0),
            preferred_element_type=F32,
            precision=lax.Precision.HIGHEST,
        )
    tgt_n[...] = ordered.astype(jnp.int32)

    rho = lax.broadcasted_iota(jnp.int32, (512, 512), 0)
    lane = lax.broadcasted_iota(jnp.int32, (512, 512), 1)
    slot = rho // 64
    plane_k = jnp.bitwise_and(jnp.where(par == 0, z - slot, z + slot), 15)
    pos = plane_k * 2048 + v * 64 + rho % 64
    diff[...] = pos - (32 * (2 * (lane % 8) + (lane // 64) % 2) + lane // 128)

    q1buf[z] = q1src[g]

    @pl.loop(1, NZ)
    def _(d):
        frm = wrap(z - d + NZ, NZ)
        got(q1buf.at[frm], q1_r.at[frm])

    ri = lax.broadcasted_iota(jnp.int32, (128, 128), 0)
    ci = lax.broadcasted_iota(jnp.int32, (128, 128), 1)
    from_row = (2 * (ri % 8) + ri // 64) * 8 + (ri // 8) % 8
    q_rows = q1buf[...].astype(F32).reshape(128, 128).astype(BF16)
    qall[v] = jnp.dot(
        (ci == from_row).astype(BF16), q_rows, preferred_element_type=F32
    ).astype(BF16)

    @pl.loop(1, NV)
    def _(k):
        o = wrap(v + k, NV)
        push(qall.at[v], qall.at[v], qa_s.at[k], qa_r.at[v], dev(z, y, o // NC, o % NC))

    def forward(buf, i, ss, rs):
        @pl.loop(0, 8)
        def _(k):
            @pl.when(k > 0)
            def _():
                got(buf.at[y, k], kv_r.at[k, i])

            for e in (1, 3, 2):
                to = dev(z, wrap(y + e, NY), x, c)
                push(buf.at[y, k], buf.at[y, k], ss.at[k, e], rs.at[y, k], to)

    own_k.wait()
    forward(kbuf, 0, kf_s, kf_r)

    @pl.loop(1, NV)
    def _(k):
        o = wrap(v + k, NV)
        got(qall.at[o], qa_r.at[o])

    span = span_m[0]
    turn = math.log2(math.e) / math.sqrt(HEAD_DIM)

    def stat_rows(top, total):
        rows = list(split3(top)) + list(split3(total))
        return jnp.concatenate(rows + [jnp.zeros((10, top.shape[1]), F32)], axis=0).astype(BF16)

    def weigh(e):
        yy = wrap(y - e + NY, NY)
        keys = kbuf[yy].reshape(512, 128)
        for i in range(2):
            scores = nt(keys, qall[4 * i : 4 * i + 4].reshape(512, 128))
            live = diff[...] <= span + 8 * y + 4 * i - 512 * yy
            scores = jnp.where(live, scores, LOW)
            top = jnp.maximum(jnp.max(scores, axis=0, keepdims=True), 0.5 * LOW)
            wts = jnp.exp2((scores - top) * turn)
            run_m[i, e, 0:1] = top
            run_m[i, e, 1:2] = jnp.sum(wts, axis=0, keepdims=True)
            wts_m[i, e] = wts.astype(BF16)

    def mix(e):
        yy = wrap(y - e + NY, NY)
        vals_t = vbuf[yy].reshape(512, 128).T
        for i in range(2):
            tops = [run_m[i, b, 0:1] for b in range(NY)]
            top = jnp.maximum(jnp.maximum(tops[0], tops[1]), jnp.maximum(tops[2], tops[3]))
            acc = jnp.dot(vals_t, wts_m[i, e], preferred_element_type=F32)
            acc = acc * jnp.exp2((tops[e] - top) * turn)
            if e > 0:
                acc = acc + acc_m[i]
            if e < NY - 1:
                acc_m[i] = acc
                continue
            total = jnp.zeros((1, 512), F32)
            for b in range(NY):
                total = total + run_m[i, b, 1:2] * jnp.exp2((tops[b] - top) * turn)
            tail = stat_rows(top, total)
            for b in range(4):
                o = 4 * i + b
                lanes = slice(b * 128, (b + 1) * 128)
                osend[o, 0:128, :] = acc[:, lanes].astype(BF16)
                osend[o, 128:144, :] = tail[:, lanes]

                @pl.when(v != o)
                def _():
                    push(osend.at[o], obuf.at[v], o_s.at[o], o_r.at[v], dev(z, y, o // NC, o % NC))

    def arrived(e, buf, rs):
        yy = wrap(y - e + NY, NY)

        @pl.loop(0, 8)
        def _(k):
            got(buf.at[yy, k], rs.at[yy, k])

    weigh(0)
    own_v.wait()
    forward(vbuf, 1, vf_s, vf_r)
    own_w.wait()
    push(wbuf.at[par, y], wbuf.at[par, y], w_s.at[0], w_r.at[par, y], dev(z + 1 - 2 * par, y, x, c))
    for e in (1, 3, 2):
        arrived(e, kbuf, kf_r)
        weigh(e)
    mix(0)
    for e in (1, 2, 3):
        arrived(e, vbuf, vf_r)
        mix(e)

    got(wbuf.at[1 - par, y], w_r.at[1 - par, y])
    for d in range(1, NY):
        there = wbuf.at[1 - par, y]
        push(there, there, wf_s.at[d], w_r.at[1 - par, y], dev(z, wrap(y + d, NY), x, c))

    def unpack_stats(tail):
        b = tail.astype(F32)
        return b[0:1] + b[1:2] + b[2:3], b[3:4] + b[4:5] + b[5:6]

    def blend(one, two):
        m1, l1, a1 = one
        m2, l2, a2 = two
        m = jnp.maximum(m1, m2)
        f1, f2 = jnp.exp2((m1 - m) * turn), jnp.exp2((m2 - m) * turn)
        return m, l1 * f1 + l2 * f2, a1 * f1 + a2 * f2

    obuf[v] = osend[v]

    @pl.loop(1, NV)
    def _(k):
        frm = wrap(v - k + NV, NV)
        got(obuf.at[frm], o_r.at[frm])

    tails = [unpack_stats(obuf[i, 128:144, :]) for i in range(NV)]
    m_own = tails[0][0]
    for m_one, _ in tails[1:]:
        m_own = jnp.maximum(m_own, m_one)
    l_own = jnp.zeros((1, 128), F32)
    a_own = jnp.zeros((128, 128), F32)
    for i, (m_one, l_one) in enumerate(tails):
        fade = jnp.exp2((m_one - m_own) * turn)
        l_own = l_own + l_one * fade
        a_own = a_own + obuf[i, 0:128, :].astype(F32) * fade

    psrc[0:128, :] = a_own.astype(BF16)
    psrc[128:144, :] = stat_rows(m_own, l_own)
    push(psrc, pbuf, p_s.at[0], p_r.at[0], dev(z + 1 - 2 * par, y, x, c))
    got(pbuf, p_r.at[0])
    m_two, l_two = unpack_stats(pbuf[128:144, :])
    _, l_all, a_all = blend(
        (m_own, l_own, a_own), (m_two, l_two, pbuf[0:128, :].astype(F32))
    )
    att[...] = (a_all / l_all).T.astype(BF16)

    mine = att.at[pl.ds(pl.multiple_of(par * 64, 64), 64)]

    @pl.loop(1, NV)
    def _(k):
        o = wrap(v + k, NV)
        push(mine, abuf.at[v], a_s.at[k], a_r.at[v], dev(z, y, o // NC, o % NC))

    abuf[v] = att[pl.ds(pl.multiple_of(par * 64, 64), 64), :]
    for d in range(1, NY):
        frm_y = wrap(y - d + NY, NY)
        got(wbuf.at[par, frm_y], w_r.at[par, frm_y])
        got(wbuf.at[1 - par, frm_y], w_r.at[1 - par, frm_y])

    @pl.loop(1, NV)
    def _(k):
        frm = wrap(v - k + NV, NV)
        got(abuf.at[frm], a_r.at[frm])

    rows_f = abuf[...].astype(F32)
    proj = jnp.zeros((64, COLS), F32)
    for h in range(8):
        rows = rows_f[:, h * 8 : (h + 1) * 8, :].reshape(64, 128).astype(BF16)
        proj = proj + jnp.dot(rows, wbuf[h // 4, h % 4], preferred_element_type=F32)
    r64 = lax.broadcasted_iota(jnp.int32, (64, 64), 0)
    c64 = lax.broadcasted_iota(jnp.int32, (64, 64), 1)
    to_planes = (c64 == (r64 % 8) * 8 + r64 // 8).astype(BF16)
    by_plane = jnp.dot(to_planes, proj.astype(BF16), preferred_element_type=F32)
    prsend[...] = by_plane.reshape(8, 8, COLS).astype(BF16)

    @pl.loop(1, 8)
    def _(d):
        to = wrap(g + d, 8)
        push(prsend.at[to], prbuf.at[g], pr_s.at[d], pr_r.at[g], dev(2 * to + par, y, x, c))

    hidden = res_m[...].astype(F32) + prsend[g].astype(F32)
    for d in range(1, 8):
        frm = wrap(g - d + 8, 8)
        got(prbuf.at[frm], pr_r.at[frm])
        hidden = hidden + prbuf[frm].astype(F32)
    hsend[...] = (hidden * gain_n[v]).astype(BF16)

    half = z // 8

    @pl.loop(1, NZ)
    def _(d):
        to = wrap(z + d, NZ)
        k = lax.rem(z + 16 - to, 8)
        push(hsend, hall.at[x, k, y, c], h_s.at[d], h_r.at[k, c], dev(to, y, x, half))

    @pl.when(c == half)
    def _():
        keep = pltpu.make_async_copy(hsend, hall.at[x, 0, y, c], h_r.at[0, c])
        keep.start()

    @pl.when(c != half)
    def _():
        push(hsend, hall.at[x, 0, y, c], h_s.at[0], h_r.at[0, c], dev(z, y, x, half))

    def block(xx, yy, i):
        return hall.at[xx, pl.ds(2 * i, 2), yy]

    def first_step(i, x_first):
        for k in (2 * i, 2 * i + 1):
            for cc in range(NC):
                got(hall.at[x, k, y, cc], h_r.at[k, cc])
        for d in (1, 3, 2):
            to = dev(z, y, wrap(x + d, NX), c) if x_first else dev(z, wrap(y + d, NY), x, c)
            here = x if x_first else y
            push(block(x, y, i), block(x, y, i), h1_s.at[i, d], h1_r.at[i, here], to)

    def second_step(i, x_first):
        for e in (0, 1, 3, 2):
            xx = wrap(x + e, NX) if x_first else x
            yy = y if x_first else wrap(y + e, NY)
            there, here = (xx, y) if x_first else (yy, x)
            if e > 0:
                got(block(xx, yy, i), h1_r.at[i, there])
            for d in (1, 3, 2):
                to = dev(z, wrap(y + d, NY), x, c) if x_first else dev(z, y, wrap(x + d, NX), c)
                push(
                    block(xx, yy, i),
                    block(xx, yy, i),
                    h2_s.at[i, e, d],
                    h2_r.at[i, here, there],
                    to,
                )

    def arrivals(i, x_first):
        for d in range(1, 4):
            for e in range(4):
                frm = wrap((y if x_first else x) + d, 4)
                xx, yy = (e, frm) if x_first else (frm, e)
                got(block(xx, yy, i), h2_r.at[i, frm, e])

    first_step(0, True)
    first_step(3, False)
    second_step(0, True)
    first_step(1, True)
    second_step(3, False)
    first_step(2, False)
    second_step(1, True)
    second_step(2, False)

    own_head.wait()
    got(whead.at[1], hw_r.at[0])
    for i, x_first in ((0, True), (3, False), (1, True), (2, False)):
        arrivals(i, x_first)

    logit[...] = jnp.zeros_like(logit)

    def head_step(n, squares):
        hid = hall[n // 2, :, :, lax.rem(n, 2)].astype(F32).reshape(256, COLS)
        inv = ginv_n[n]
        for t in range(COLS // 128):
            part = hid[:, t * 128 : (t + 1) * 128]
            squares = squares + part * part * inv[0:1, t * 128 : (t + 1) * 128]
        hid16 = hid.astype(BF16)
        cols = pl.ds(pl.multiple_of(n * COLS, 128), COLS)
        for p in range(2):
            logit[p] += nt(whead[p, :, cols], hid16)
        return squares

    squares = lax.fori_loop(0, NV, head_step, jnp.zeros((256, 128), F32))
    sums = nt(jnp.ones((8, 128), F32), squares, lax.Precision.HIGHEST)
    row_scale = lax.rsqrt(sums[0:1] / WIDTH + FLOOR)
    targets = tgt_n[0:1]
    row_id = lax.broadcasted_iota(jnp.int32, (ROWS, 256), 0)
    tops, parts, picks = [], [], []
    for p in range(2):
        block = s * NV + (v if p == 0 else v + 1 - 2 * c)
        lg = logit[p] * row_scale
        logit[p] = lg
        picks.append(
            jnp.sum(jnp.where(row_id == targets - block * ROWS, lg, 0.0), axis=0, keepdims=True)
        )
        tops.append(jnp.max(lg, axis=0, keepdims=True))
    top = jnp.maximum(tops[0], tops[1])
    for p in range(2):
        parts.append(jnp.sum(jnp.exp(logit[p] - top), axis=0, keepdims=True))
    stats = jnp.concatenate(
        [top, parts[0] + parts[1], picks[0] + picks[1], jnp.zeros((5, 256), F32)], axis=0
    )
    stsrc[...] = jnp.zeros_like(stsrc)
    for k in range(8):
        stsrc[k, :, 0:32] = stats[:, k * 32 : (k + 1) * 32]

    def join_all(ref, n):
        m = ref[0, 0:1]
        for i in range(1, n):
            m = jnp.maximum(m, ref[i, 0:1])
        t = jnp.zeros_like(m)
        picked = jnp.zeros_like(m)
        for i in range(n):
            t = t + ref[i, 1:2] * jnp.exp(ref[i, 0:1] - m)
            picked = picked + ref[i, 2:3]
        return m, t, picked

    @pl.loop(0, 8)
    def _(k):
        to = 8 * c + lax.rem(z + k, 8)

        @pl.when(to != z)
        def _():
            push(stsrc.at[k], stz.at[z], t1_s.at[k], t1_r.at[z], dev(to, y, x, c))

    @pl.when(c == half)
    def _():
        stz[z] = stsrc[0]

        @pl.loop(1, NZ)
        def _(d):
            frm = wrap(z + d, NZ)
            got(stz.at[frm], t1_r.at[frm])

        m, t, picked = join_all(stz, NZ)
        stred[...] = jnp.concatenate([m, t, picked, jnp.zeros((5, 128), F32)], axis=0)

        push(stred, stfin.at[q], t2_s.at[0, 0], t2_r.at[q], dev(z, y, x, 1 - c))
        for k in (1, 4, 3, 12, 2, 8, 5, 15, 6, 9, 7, 13, 10, 11, 14):
            for cc in range(NC):
                to = dev(z, flip(y, k // 4), flip(x, k % 4), cc)
                push(stred, stfin.at[q], t2_s.at[k, cc], t2_r.at[q], to)
        stfin[q] = stred[...]

    @pl.when(c != half)
    def _():
        got(stfin.at[q], t2_r.at[q])

    for k in range(1, 16):
        o = flip(y, k // 4) * NX + flip(x, k % 4)
        got(stfin.at[o], t2_r.at[o])

    m, t, picked = join_all(stfin, 16)
    logprob = picked - m - jnp.log(t)
    shift = lax.rem(128 - y * 8, 128)
    out_ref[...] = pltpu.roll(jnp.broadcast_to(logprob, (8, 128)), shift, 1)

    @pl.loop(1, NZ)
    def _(d):
        got(q1src.at[0], q1_s.at[d])
        got(hsend, h_s.at[d])

    @pl.when(c != half)
    def _():
        got(hsend, h_s.at[0])

    @pl.loop(1, 8)
    def _(d):
        got(kbuf.at[0, 0], kv_s.at[d, 0])
        got(vbuf.at[0, 0], kv_s.at[d, 1])
        got(qall.at[0], qa_s.at[d])
        got(prsend.at[0], pr_s.at[d])
        got(abuf.at[0], a_s.at[d])

    @pl.loop(0, NV)
    def _(o):
        @pl.when(o != v)
        def _():
            got(osend.at[0], o_s.at[o])

    got(wbuf.at[0, 0], w_s.at[0])
    for d in range(1, NY):
        got(wbuf.at[0, 0], w_s.at[d])
        got(wbuf.at[0, 0], wf_s.at[d])

        @pl.loop(0, 8)
        def _(k):
            got(kbuf.at[0, 0], kf_s.at[k, d])
            got(vbuf.at[0, 0], vf_s.at[k, d])

    got(whead.at[1], hw_s.at[0])
    got(psrc, p_s.at[0])

    @pl.loop(0, 4)
    def _(i):
        for d in range(1, 4):
            got(hall.at[0, pl.ds(0, 2), 0], h1_s.at[i, d])
            for e in range(4):
                got(hall.at[0, pl.ds(0, 2), 0], h2_s.at[i, e, d])

    @pl.loop(0, 8)
    def _(k):
        @pl.when(8 * c + lax.rem(z + k, 8) != z)
        def _():
            got(stsrc.at[0], t1_s.at[k])

    @pl.when(c == half)
    def _():
        got(stred, t2_s.at[0, 0])

        @pl.loop(1, 16)
        def _(k):
            for cc in range(NC):
                got(stred, t2_s.at[k, cc])


def body(
    queries,
    cached_keys,
    cached_values,
    out_weight,
    residual,
    norm_gain,
    head_weight,
    targets,
    span_offset,
):
    vm = pl.BlockSpec(memory_space=pltpu.VMEM)
    hbm = pl.BlockSpec(memory_space=pl.ANY)
    dma = pltpu.SemaphoreType.DMA
    out = pl.pallas_call(
        kernel,
        out_shape=jax.ShapeDtypeStruct((8, 128), F32),
        in_specs=[hbm] * 9,
        out_specs=vm,
        scratch_shapes=[
            pltpu.SMEM((1,), jnp.int32),
            pltpu.VMEM((8, 64 * HEAD_DIM), BF16),
            pltpu.VMEM((8, COLS), BF16),
            pltpu.VMEM((WIDTH,), BF16),
            pltpu.VMEM((512,), jnp.int32),
            pltpu.VMEM((NV, 1, COLS), F32),
            pltpu.VMEM((NV, 8, COLS), F32),
            pltpu.VMEM((8, 256), jnp.int32),
            pltpu.VMEM((512, 512), jnp.int32),
            pltpu.VMEM((8, 8, 128), BF16),
            pltpu.VMEM((NZ, 8, 128), BF16),
            pltpu.VMEM((NV, 128, 128), BF16),
            pltpu.VMEM((NY, 8, 64, 128), BF16),
            pltpu.VMEM((NY, 8, 64, 128), BF16),
            pltpu.VMEM((2, NY, 512, 512), BF16),
            pltpu.VMEM((2, 128, 512), F32),
            pltpu.VMEM((2, NY, 8, 512), F32),
            pltpu.VMEM((NV, 144, 128), BF16),
            pltpu.VMEM((NV, 144, 128), BF16),
            pltpu.VMEM((144, 128), BF16),
            pltpu.VMEM((144, 128), BF16),
            pltpu.VMEM((128, 128), BF16),
            pltpu.VMEM((NV, 64, 128), BF16),
            pltpu.VMEM((2, NY, 128, COLS), BF16),
            pltpu.VMEM((8, 8, COLS), BF16),
            pltpu.VMEM((8, 8, COLS), BF16),
            pltpu.VMEM((8, COLS), BF16),
            pltpu.VMEM((NX, 8, NY, NC, 8, COLS), BF16),
            pltpu.VMEM((2, ROWS, WIDTH), BF16),
            pltpu.VMEM((2, ROWS, 256), F32),
            pltpu.VMEM((8, 8, 128), F32),
            pltpu.VMEM((NZ, 8, 128), F32),
            pltpu.VMEM((8, 128), F32),
            pltpu.VMEM((16, 8, 128), F32),
            dma((8, 2)),
            dma((8, 2)),
            dma((8, NY)),
            dma((8, NY)),
            dma((NY, 8)),
            dma((NY, 8)),
            dma((NZ,)),
            dma((NZ,)),
            dma((NV,)),
            dma((NV,)),
            dma((NV,)),
            dma((NV,)),
            dma((1,)),
            dma((1,)),
            dma((NV,)),
            dma((NV,)),
            dma((NY,)),
            dma((2, NY)),
            dma((NY,)),
            dma((8,)),
            dma((8,)),
            dma((NZ,)),
            dma((8, NC)),
            dma((4, 4)),
            dma((4, 4)),
            dma((4, 4, 4)),
            dma((4, 4, 4)),
            dma((1,)),
            dma((1,)),
            dma((8,)),
            dma((NZ,)),
            dma((16, NC)),
            dma((16,)),
            dma((9,)),
        ],
        compiler_params=pltpu.CompilerParams(
            collective_id=0, has_side_effects=True, vmem_limit_bytes=60 * 2**20
        ),
        cost_estimate=pl.CostEstimate(
            flops=3_000_000_000, bytes_accessed=8_000_000, transcendentals=2_500_000
        ),
    )(
        span_offset,
        queries,
        cached_keys,
        cached_values,
        out_weight,
        residual,
        norm_gain,
        head_weight,
        targets,
    )
    return out[0, :8]


def solution(mesh):
    return jax.shard_map(
        body,
        mesh=mesh,
        in_specs=(
            P("seq", None),
            P(("seq", "vocab"), None),
            P(("seq", "vocab"), None),
            P("seq", "vocab"),
            P("seq", "vocab"),
            P(),
            P(("seq", "vocab"), None),
            P(),
            P(),
        ),
        out_specs=P("seq"),
        check_vma=False,
    )
```

```python
import math

import jax
import jax.numpy as jnp
from jax import lax
from jax.experimental import pallas as pl
from jax.experimental.pallas import tpu as pltpu
from jax.sharding import PartitionSpec as P

MESH = pl.DeviceIdType.MESH
HEAD_DIM = 128
NZ, NY, NX, NC = 16, 4, 4, 2
NV = NX * NC
WIDTH = 5120
COLS = WIDTH // NV
ROWS = 296
FLOOR = 1e-06
LOW = -1e30
F32 = jnp.float32
BF16 = jnp.bfloat16


def split3(x):
    hi = x.astype(BF16).astype(F32)
    rest = x - hi
    mid = rest.astype(BF16).astype(F32)
    lo = (rest - mid).astype(BF16).astype(F32)
    return hi, mid, lo


def nt(a, b, precision=None):
    return lax.dot_general(
        a, b, (((1,), (1,)), ((), ())), preferred_element_type=F32, precision=precision
    )


def kernel(
    span_ref,
    q_ref,
    k_ref,
    v_ref,
    w_ref,
    res_ref,
    gain_ref,
    head_ref,
    tgt_ref,
    out_ref,
    span_m,
    q_m,
    res_m,
    gain_m,
    tgt_m,
    gain_n,
    ginv_n,
    tgt_n,
    diff,
    q1src,
    q1buf,
    qall,
    kbuf,
    vbuf,
    wts_m,
    acc_m,
    run_m,
    osend,
    obuf,
    psrc,
    pbuf,
    att,
    abuf,
    wbuf,
    prsend,
    prbuf,
    hsend,
    hall,
    whead,
    hid_m,
    sq_m,
    logit,
    stsrc,
    stz,
    stred,
    stfin,
    kv_s,
    kv_r,
    kf_s,
    vf_s,
    kf_r,
    vf_r,
    q1_s,
    q1_r,
    qa_s,
    qa_r,
    o_s,
    o_r,
    p_s,
    p_r,
    a_s,
    a_r,
    w_s,
    w_r,
    wf_s,
    pr_s,
    pr_r,
    h_s,
    h_r,
    h1_s,
    h1_r,
    h2_s,
    h2_r,
    h3_s,
    h3_r,
    hw_s,
    hw_r,
    t1_s,
    t1_r,
    t2_s,
    t2_r,
    loc,
):
    s = lax.axis_index("seq")
    v = lax.axis_index("vocab")
    z, y, x, c = s // NY, s % NY, v // NC, v % NC
    g, par = z // 2, z % 2
    half = z // 8
    z_low = z - 8 * half
    q = y * NX + x

    def dev(zz, yy, xx, cc):
        return (zz * NY + yy, xx * NC + cc)

    def wrap(a, n):
        return jnp.where(a >= n, a - n, a)

    def flips(a):
        odd = a % 2
        return (a, a + 1 - 2 * odd, wrap(a + 2, 4), 3 - a)

    flip_x, flip_y = flips(x), flips(y)

    def push(src, dst, ss, rs, to):
        cp = pltpu.make_async_remote_copy(
            src_ref=src, dst_ref=dst, send_sem=ss, recv_sem=rs, device_id=to, device_id_type=MESH
        )
        cp.start()

    def got(ref, sem):
        pltpu.make_async_copy(ref, ref, sem).wait()

    own_head = pltpu.make_async_copy(head_ref, whead.at[0], loc.at[0])
    own_head.start()
    own_w = pltpu.make_async_copy(w_ref, wbuf.at[par, y], loc.at[1])
    own_w.start()
    own_k = pltpu.make_async_copy(
        k_ref.at[:, pl.ds(pl.multiple_of(g * 128, 128), 128)], kbuf.at[y, 0], loc.at[2]
    )
    own_k.start()
    own_v = pltpu.make_async_copy(
        v_ref.at[:, pl.ds(pl.multiple_of(g * 128, 128), 128)], vbuf.at[y, 0], loc.at[3]
    )
    own_v.start()
    loads = [
        pltpu.make_async_copy(a, b, loc.at[4 + i])
        for i, (a, b) in enumerate(
            (
                (q_ref, q_m),
                (gain_ref, gain_m),
                (tgt_ref, tgt_m),
                (span_ref, span_m),
                (res_ref, res_m),
            )
        )
    ]
    for cp in loads:
        cp.start()

    barrier = pltpu.get_barrier_semaphore()

    def greet(zz, yy, xx, cc):
        pl.semaphore_signal(barrier, inc=1, device_id=dev(zz, yy, xx, cc), device_id_type=MESH)

    @pl.loop(1, NZ)
    def _(d):
        greet(wrap(z + d, NZ), y, x, c)
        greet(wrap(z + d, NZ), y, x, 1 - c)

    greet(z, y, x, 1 - c)
    for k in range(1, 16):
        for cc in range(NC):
            greet(z, flip_y[k // 4], flip_x[k % 4], cc)

    for cp in loads:
        cp.wait()
    q_f = q_m[...].astype(F32)
    pick_row = lax.broadcasted_iota(jnp.int32, (8, 128), 0) == v
    for gg in range(8):
        rows = []
        for h in range(8 * gg, 8 * gg + 8):
            part = jnp.where(pick_row, q_f[:, h * 128 : (h + 1) * 128], 0.0)
            rows.append(jnp.sum(part, axis=0, keepdims=True))
        q1src[gg] = jnp.concatenate(rows, axis=0).astype(BF16)

    pl.semaphore_wait(barrier, 2 * (NZ - 1) + 31)

    @pl.loop(1, NZ)
    def _(d):
        to = wrap(z + d, NZ)
        push(q1src.at[to // 2], q1buf.at[z], q1_s.at[d], q1_r.at[z], dev(to, y, x, c))

    def spread(src, dst, i):
        @pl.loop(1, 8)
        def _(d):
            head = wrap(g + d, 8)
            ahead = 2 * d - par
            up = ahead <= 7
            to = dev(2 * head + jnp.where(up, 0, 1), y, x, c)
            k = jnp.where(up, ahead, 15 - ahead)
            cols = pl.ds(pl.multiple_of(head * 128, 128), 128)
            push(src.at[:, cols], dst.at[y, k], kv_s.at[d, i], kv_r.at[k, i], to)

    spread(k_ref, kbuf, 0)

    for d in range(1, NY):
        push(w_ref, wbuf.at[par, y], w_s.at[d], w_r.at[par, y], dev(z, wrap(y + d, NY), x, c))
    push(head_ref, whead.at[1], hw_s.at[0], hw_r.at[0], dev(z, y, x, 1 - c))

    gains = gain_m[...].astype(F32).reshape(WIDTH // 128, 128)
    for t in range(WIDTH // 128):
        one = gains[t : t + 1]
        lanes = slice((t % 5) * 128, (t % 5 + 1) * 128)
        gain_n[t // 5, :, lanes] = one
        ginv_n[t // 5, :, lanes] = jnp.broadcast_to(1.0 / (one * one), (8, 128))
    tgt4 = tgt_m[...].reshape(4, 128).astype(F32)
    src = lax.broadcasted_iota(jnp.int32, (128, 256), 0)
    dst = lax.broadcasted_iota(jnp.int32, (128, 256), 1)
    plane_of = lax.rem((dst // 8) % 8 + z, 8)
    here = src == (plane_of % 4) * 32 + (dst // 64) * 8 + dst % 8
    ordered = jnp.zeros((8, 256), F32)
    for r in range(2):
        row = jnp.where(c == 0, tgt4[r : r + 1], tgt4[2 + r : 3 + r])
        ordered = ordered + jnp.dot(
            jnp.broadcast_to(row, (8, 128)),
            jnp.where(here & (plane_of // 4 == r), 1.0, 0.0),
            preferred_element_type=F32,
            precision=lax.Precision.HIGHEST,
        )
    tgt_n[...] = ordered.astype(jnp.int32)

    rho = lax.broadcasted_iota(jnp.int32, (512, 512), 0)
    lane = lax.broadcasted_iota(jnp.int32, (512, 512), 1)
    slot = rho // 64
    plane_k = jnp.bitwise_and(jnp.where(par == 0, z - slot, z + slot), 15)
    pos = plane_k * 2048 + v * 64 + rho % 64
    diff[...] = pos - (32 * (2 * (lane % 8) + (lane // 64) % 2) + lane // 128)

    q1buf[z] = q1src[g]

    @pl.loop(1, NZ)
    def _(d):
        frm = wrap(z - d + NZ, NZ)
        got(q1buf.at[frm], q1_r.at[frm])

    ri = lax.broadcasted_iota(jnp.int32, (128, 128), 0)
    ci = lax.broadcasted_iota(jnp.int32, (128, 128), 1)
    from_row = (2 * (ri % 8) + ri // 64) * 8 + (ri // 8) % 8
    q_rows = q1buf[...].astype(F32).reshape(128, 128).astype(BF16)
    qall[v] = jnp.dot(
        (ci == from_row).astype(BF16), q_rows, preferred_element_type=F32
    ).astype(BF16)

    @pl.loop(1, 8)
    def _(d):
        got(kbuf.at[0, 0], kv_s.at[d, 0])

    spread(v_ref, vbuf, 1)

    @pl.loop(1, NV)
    def _(k):
        o = wrap(v + k, NV)
        push(qall.at[v], qall.at[v], qa_s.at[k], qa_r.at[v], (s, o))

    def forward(buf, i, ss, rs):
        @pl.loop(0, 8)
        def _(k):
            @pl.when(k > 0)
            def _():
                got(buf.at[y, k], kv_r.at[k, i])

            for e in (1, 3, 2):
                to = dev(z, wrap(y + e, NY), x, c)
                push(buf.at[y, k], buf.at[y, k], ss.at[k, e], rs.at[y, k], to)

    own_k.wait()
    forward(kbuf, 0, kf_s, kf_r)

    @pl.loop(1, NV)
    def _(k):
        o = wrap(v + k, NV)
        got(qall.at[o], qa_r.at[o])

    span = span_m[0]
    turn = math.log2(math.e) / math.sqrt(HEAD_DIM)

    def stat_rows(top, total):
        rows = list(split3(top)) + list(split3(total))
        return jnp.concatenate(rows + [jnp.zeros((10, top.shape[1]), F32)], axis=0).astype(BF16)

    def weigh(e):
        yy = wrap(y - e + NY, NY)
        keys = kbuf[yy].reshape(512, 128)
        for i in range(2):
            scores = nt(keys, qall[4 * i : 4 * i + 4].reshape(512, 128))
            live = diff[...] <= span + 8 * y + 4 * i - 512 * yy
            scores = jnp.where(live, scores, LOW)
            top = jnp.maximum(jnp.max(scores, axis=0, keepdims=True), 0.5 * LOW)
            wts = jnp.exp2((scores - top) * turn)
            run_m[i, e, 0:1] = top
            run_m[i, e, 1:2] = jnp.sum(wts, axis=0, keepdims=True)
            wts_m[i, e] = wts.astype(BF16)

    def mix(e):
        yy = wrap(y - e + NY, NY)
        vals_t = vbuf[yy].reshape(512, 128).T
        for i in range(2):
            tops = [run_m[i, b, 0:1] for b in range(NY)]
            top = jnp.maximum(jnp.maximum(tops[0], tops[1]), jnp.maximum(tops[2], tops[3]))
            acc = jnp.dot(vals_t, wts_m[i, e], preferred_element_type=F32)
            acc = acc * jnp.exp2((tops[e] - top) * turn)
            if e > 0:
                acc = acc + acc_m[i]
            if e < NY - 1:
                acc_m[i] = acc
                continue
            total = jnp.zeros((1, 512), F32)
            for b in range(NY):
                total = total + run_m[i, b, 1:2] * jnp.exp2((tops[b] - top) * turn)
            tail = stat_rows(top, total)
            for b in range(4):
                o = 4 * i + b
                lanes = slice(b * 128, (b + 1) * 128)
                osend[o, 0:128, :] = acc[:, lanes].astype(BF16)
                osend[o, 128:144, :] = tail[:, lanes]

                @pl.when(v != o)
                def _():
                    push(osend.at[o], obuf.at[v], o_s.at[o], o_r.at[v], (s, o))

    def arrived(e, buf, rs):
        yy = wrap(y - e + NY, NY)

        @pl.loop(0, 8)
        def _(k):
            got(buf.at[yy, k], rs.at[yy, k])

    weigh(0)
    own_v.wait()
    forward(vbuf, 1, vf_s, vf_r)
    own_w.wait()
    push(wbuf.at[par, y], wbuf.at[par, y], w_s.at[0], w_r.at[par, y], dev(z + 1 - 2 * par, y, x, c))
    for e in (1, 3, 2):
        arrived(e, kbuf, kf_r)
        weigh(e)
    mix(0)
    for e in (1, 2, 3):
        arrived(e, vbuf, vf_r)
        mix(e)

    got(wbuf.at[1 - par, y], w_r.at[1 - par, y])
    for d in range(1, NY):
        there = wbuf.at[1 - par, y]
        push(there, there, wf_s.at[d], w_r.at[1 - par, y], dev(z, wrap(y + d, NY), x, c))

    def unpack_stats(tail):
        b = tail.astype(F32)
        return b[0:1] + b[1:2] + b[2:3], b[3:4] + b[4:5] + b[5:6]

    def blend(one, two):
        m1, l1, a1 = one
        m2, l2, a2 = two
        m = jnp.maximum(m1, m2)
        f1, f2 = jnp.exp2((m1 - m) * turn), jnp.exp2((m2 - m) * turn)
        return m, l1 * f1 + l2 * f2, a1 * f1 + a2 * f2

    obuf[v] = osend[v]

    @pl.loop(1, NV)
    def _(k):
        frm = wrap(v - k + NV, NV)
        got(obuf.at[frm], o_r.at[frm])

    tails = [unpack_stats(obuf[i, 128:144, :]) for i in range(NV)]
    m_own = tails[0][0]
    for m_one, _ in tails[1:]:
        m_own = jnp.maximum(m_own, m_one)
    l_own = jnp.zeros((1, 128), F32)
    a_own = jnp.zeros((128, 128), F32)
    for i, (m_one, l_one) in enumerate(tails):
        fade = jnp.exp2((m_one - m_own) * turn)
        l_own = l_own + l_one * fade
        a_own = a_own + obuf[i, 0:128, :].astype(F32) * fade

    psrc[0:128, :] = a_own.astype(BF16)
    psrc[128:144, :] = stat_rows(m_own, l_own)
    push(psrc, pbuf, p_s.at[0], p_r.at[0], dev(z + 1 - 2 * par, y, x, c))
    got(pbuf, p_r.at[0])
    m_two, l_two = unpack_stats(pbuf[128:144, :])
    _, l_all, a_all = blend(
        (m_own, l_own, a_own), (m_two, l_two, pbuf[0:128, :].astype(F32))
    )
    att[...] = (a_all / l_all).T.astype(BF16)

    mine = att.at[pl.ds(pl.multiple_of(par * 64, 64), 64)]

    @pl.loop(1, NV)
    def _(k):
        o = wrap(v + k, NV)
        push(mine, abuf.at[v], a_s.at[k], a_r.at[v], (s, o))

    abuf[v] = att[pl.ds(pl.multiple_of(par * 64, 64), 64), :]
    for d in range(1, NY):
        frm_y = wrap(y - d + NY, NY)
        got(wbuf.at[par, frm_y], w_r.at[par, frm_y])
        got(wbuf.at[1 - par, frm_y], w_r.at[1 - par, frm_y])

    @pl.loop(1, NV)
    def _(k):
        frm = wrap(v - k + NV, NV)
        got(abuf.at[frm], a_r.at[frm])

    rows_f = abuf[...].astype(F32)
    proj = jnp.zeros((64, COLS), F32)
    for h in range(8):
        rows = rows_f[:, h * 8 : (h + 1) * 8, :].reshape(64, 128).astype(BF16)
        proj = proj + jnp.dot(rows, wbuf[h // 4, h % 4], preferred_element_type=F32)
    r64 = lax.broadcasted_iota(jnp.int32, (64, 64), 0)
    c64 = lax.broadcasted_iota(jnp.int32, (64, 64), 1)
    to_planes = (c64 == (r64 % 8) * 8 + r64 // 8).astype(BF16)
    by_plane = jnp.dot(to_planes, proj.astype(BF16), preferred_element_type=F32)
    prsend[...] = by_plane.reshape(8, 8, COLS).astype(BF16)

    @pl.loop(1, 8)
    def _(d):
        to = wrap(g + d, 8)
        push(prsend.at[to], prbuf.at[g], pr_s.at[d], pr_r.at[g], dev(2 * to + par, y, x, c))

    hidden = res_m[...].astype(F32) + prsend[g].astype(F32)
    for d in range(1, 8):
        frm = wrap(g - d + 8, 8)
        got(prbuf.at[frm], pr_r.at[frm])
        hidden = hidden + prbuf[frm].astype(F32)
    hsend[...] = (hidden * gain_n[v]).astype(BF16)

    @pl.loop(1, NZ)
    def _(d):
        to = wrap(z + d, NZ)
        k = wrap(wrap(z_low - to + 16, 16), 8)
        slot = hall.at[k // 4, x, y, k % 4, c]
        push(hsend, slot, h_s.at[d], h_r.at[k, c], dev(to, y, x, half))

    @pl.when(c == half)
    def _():
        keep = pltpu.make_async_copy(hsend, hall.at[0, x, y, 0, c], h_r.at[0, c])
        keep.start()

    @pl.when(c != half)
    def _():
        push(hsend, hall.at[0, x, y, 0, c], h_s.at[0], h_r.at[0, c], dev(z, y, x, half))

    def piece(i, a, b):
        xx, yy = (a, b) if i == 0 else (b, a)
        return hall.at[i, xx, yy]

    def first_dev(i, d):
        return dev(z, y, wrap(x + d, NX), c) if i == 0 else dev(z, wrap(y + d, NY), x, c)

    def second_dev(i, d):
        return dev(z, wrap(y + d, NY), x, c) if i == 0 else dev(z, y, wrap(x + d, NX), c)

    def settle(i, xx, yy):
        rows = pl.ds(pl.multiple_of(yy * 64 + i * 32, 32), 32)
        squares = jnp.zeros((32, 128), F32)
        for cc in range(NC):
            hid = hall[i, xx, yy, :, cc].astype(F32).reshape(32, COLS)
            n = xx * NC + cc
            inv = ginv_n[n]
            for t in range(COLS // 128):
                part = hid[:, t * 128 : (t + 1) * 128]
                squares = squares + part * part * inv[0:1, t * 128 : (t + 1) * 128]
            cols = pl.ds(pl.multiple_of(n * COLS, 128), COLS)
            hid_m[rows, cols] = hid.astype(BF16)
        sq_m[rows, :] += squares

    def settle_line(i, b):
        @pl.loop(0, 4)
        def _(a):
            if i == 0:
                settle(i, a, b)
            else:
                settle(i, b, a)

    sq_m[...] = jnp.zeros_like(sq_m)
    lead, cross = (x, y), (y, x)
    for i in range(2):
        for k in range(4 * i, 4 * i + 4):
            for cc in range(NC):
                got(hall.at[k // 4, x, y, k % 4, cc], h_r.at[k, cc])
        for d in (1, 3, 2):
            own = piece(i, lead[i], cross[i])
            push(own, own, h1_s.at[i, d], h1_r.at[i, lead[i]], first_dev(i, d))

    def send_second(i, a, up):
        own = piece(i, a, cross[i])
        push(own, own, h2_s.at[i, a, up], h2_r.at[i, a, up], second_dev(i, 1 if up else 3))

    for a, up in ((0, 0), (2, 1), (1, 0), (3, 1)):
        for i in range(2):

            @pl.when(lead[i] != a)
            def _():
                got(piece(i, a, cross[i]), h1_r.at[i, a])

            send_second(i, a, up)
    for a, up in ((0, 1), (2, 0), (1, 1), (3, 0)):
        for i in range(2):
            send_second(i, a, up)

    for a, up in ((0, 0), (2, 1), (1, 0), (3, 1)):
        for i in range(2):
            frm = wrap(cross[i] + (3 if up else 1), 4)
            there = piece(i, a, frm)
            got(there, h2_r.at[i, a, up])
            push(there, there, h3_s.at[i, a], h3_r.at[i, a], second_dev(i, 1 if up else 3))

    for i in range(2):
        settle_line(i, cross[i])
    for i in range(2):
        for a, up in ((0, 1), (2, 0), (1, 1), (3, 0)):
            got(piece(i, a, wrap(cross[i] + (3 if up else 1), 4)), h2_r.at[i, a, up])
        settle_line(i, wrap(cross[i] + 1, 4))
        settle_line(i, wrap(cross[i] + 3, 4))
    own_head.wait()
    got(whead.at[1], hw_r.at[0])
    for i in range(2):
        for a in range(4):
            got(piece(i, a, wrap(cross[i] + 2, 4)), h3_r.at[i, a])
        settle_line(i, wrap(cross[i] + 2, 4))

    for p in range(2):
        logit[p] = nt(whead[p], hid_m[...])

    sums = nt(jnp.ones((8, 128), F32), sq_m[...], lax.Precision.HIGHEST)
    row_scale = lax.rsqrt(sums[0:1] / WIDTH + FLOOR)
    targets = tgt_n[0:1]
    row_id = lax.broadcasted_iota(jnp.int32, (ROWS, 256), 0)
    tops, parts, picks = [], [], []
    for p in range(2):
        block = s * NV + (v if p == 0 else v + 1 - 2 * c)
        lg = logit[p] * row_scale
        logit[p] = lg
        picks.append(
            jnp.sum(jnp.where(row_id == targets - block * ROWS, lg, 0.0), axis=0, keepdims=True)
        )
        tops.append(jnp.max(lg, axis=0, keepdims=True))
    top = jnp.maximum(tops[0], tops[1])
    for p in range(2):
        parts.append(jnp.sum(jnp.exp(logit[p] - top), axis=0, keepdims=True))
    stats = jnp.concatenate(
        [top, parts[0] + parts[1], picks[0] + picks[1], jnp.zeros((5, 256), F32)], axis=0
    )
    stsrc[...] = jnp.zeros_like(stsrc)
    for k in range(8):
        for yy in range(NY):
            first = yy * 64 + k * 8
            stsrc[k, :, yy * 8 : (yy + 1) * 8] = stats[:, first : first + 8]

    def join_all(ref, n):
        m = ref[0, 0:1]
        for i in range(1, n):
            m = jnp.maximum(m, ref[i, 0:1])
        t = jnp.zeros_like(m)
        picked = jnp.zeros_like(m)
        for i in range(n):
            t = t + ref[i, 1:2] * jnp.exp(ref[i, 0:1] - m)
            picked = picked + ref[i, 2:3]
        return m, t, picked

    @pl.loop(0, 8)
    def _(k):
        to = 8 * c + wrap(z_low + k, 8)

        @pl.when(to != z)
        def _():
            push(stsrc.at[k], stz.at[z], t1_s.at[k], t1_r.at[z], dev(to, y, x, c))

    @pl.when(c == half)
    def _():
        stz[z] = stsrc[0]

        @pl.loop(1, NZ)
        def _(d):
            frm = wrap(z + d, NZ)
            got(stz.at[frm], t1_r.at[frm])

        m, t, picked = join_all(stz, NZ)
        stred[...] = jnp.concatenate([m, t, picked, jnp.zeros((5, 128), F32)], axis=0)

        push(stred, stfin.at[q], t2_s.at[0, 0], t2_r.at[q], dev(z, y, x, 1 - c))
        for k in (1, 4, 3, 12, 2, 8, 5, 15, 6, 9, 7, 13, 10, 11, 14):
            for cc in range(NC):
                to = dev(z, flip_y[k // 4], flip_x[k % 4], cc)
                push(stred, stfin.at[q], t2_s.at[k, cc], t2_r.at[q], to)
        stfin[q] = stred[...]

    @pl.when(c != half)
    def _():
        got(stfin.at[q], t2_r.at[q])

    for k in range(1, 16):
        o = flip_y[k // 4] * NX + flip_x[k % 4]
        got(stfin.at[o], t2_r.at[o])

    m, t, picked = join_all(stfin, 16)
    logprob = picked - m - jnp.log(t)
    shift = lax.rem(128 - y * 8, 128)
    out_ref[...] = pltpu.roll(jnp.broadcast_to(logprob, (8, 128)), shift, 1)

    @pl.loop(1, NZ)
    def _(d):
        got(q1src.at[0], q1_s.at[d])
        got(hsend, h_s.at[d])

    @pl.when(c != half)
    def _():
        got(hsend, h_s.at[0])

    @pl.loop(1, 8)
    def _(d):
        got(vbuf.at[0, 0], kv_s.at[d, 1])
        got(qall.at[0], qa_s.at[d])
        got(prsend.at[0], pr_s.at[d])
        got(abuf.at[0], a_s.at[d])

    @pl.loop(0, NV)
    def _(o):
        @pl.when(o != v)
        def _():
            got(osend.at[0], o_s.at[o])

    got(wbuf.at[0, 0], w_s.at[0])
    for d in range(1, NY):
        got(wbuf.at[0, 0], w_s.at[d])
        got(wbuf.at[0, 0], wf_s.at[d])

        @pl.loop(0, 8)
        def _(k):
            got(kbuf.at[0, 0], kf_s.at[k, d])
            got(vbuf.at[0, 0], vf_s.at[k, d])

    got(whead.at[1], hw_s.at[0])
    got(psrc, p_s.at[0])

    for i in range(2):
        for d in range(1, 4):
            got(piece(i, 0, 0), h1_s.at[i, d])
        for a in range(4):
            got(piece(i, 0, 0), h2_s.at[i, a, 0])
            got(piece(i, 0, 0), h2_s.at[i, a, 1])
            got(piece(i, 0, 0), h3_s.at[i, a])

    @pl.loop(0, 8)
    def _(k):
        @pl.when(8 * c + wrap(z_low + k, 8) != z)
        def _():
            got(stsrc.at[0], t1_s.at[k])

    @pl.when(c == half)
    def _():
        got(stred, t2_s.at[0, 0])

        @pl.loop(1, 16)
        def _(k):
            for cc in range(NC):
                got(stred, t2_s.at[k, cc])


def body(
    queries,
    cached_keys,
    cached_values,
    out_weight,
    residual,
    norm_gain,
    head_weight,
    targets,
    span_offset,
):
    vm = pl.BlockSpec(memory_space=pltpu.VMEM)
    hbm = pl.BlockSpec(memory_space=pl.ANY)
    dma = pltpu.SemaphoreType.DMA
    out = pl.pallas_call(
        kernel,
        out_shape=jax.ShapeDtypeStruct((8, 128), F32),
        in_specs=[hbm] * 9,
        out_specs=vm,
        scratch_shapes=[
            pltpu.SMEM((1,), jnp.int32),
            pltpu.VMEM((8, 64 * HEAD_DIM), BF16),
            pltpu.VMEM((8, COLS), BF16),
            pltpu.VMEM((WIDTH,), BF16),
            pltpu.VMEM((512,), jnp.int32),
            pltpu.VMEM((NV, 1, COLS), F32),
            pltpu.VMEM((NV, 8, COLS), F32),
            pltpu.VMEM((8, 256), jnp.int32),
            pltpu.VMEM((512, 512), jnp.int32),
            pltpu.VMEM((8, 8, 128), BF16),
            pltpu.VMEM((NZ, 8, 128), BF16),
            pltpu.VMEM((NV, 128, 128), BF16),
            pltpu.VMEM((NY, 8, 64, 128), BF16),
            pltpu.VMEM((NY, 8, 64, 128), BF16),
            pltpu.VMEM((2, NY, 512, 512), BF16),
            pltpu.VMEM((2, 128, 512), F32),
            pltpu.VMEM((2, NY, 8, 512), F32),
            pltpu.VMEM((NV, 144, 128), BF16),
            pltpu.VMEM((NV, 144, 128), BF16),
            pltpu.VMEM((144, 128), BF16),
            pltpu.VMEM((144, 128), BF16),
            pltpu.VMEM((128, 128), BF16),
            pltpu.VMEM((NV, 64, 128), BF16),
            pltpu.VMEM((2, NY, 128, COLS), BF16),
            pltpu.VMEM((8, 8, COLS), BF16),
            pltpu.VMEM((8, 8, COLS), BF16),
            pltpu.VMEM((8, COLS), BF16),
            pltpu.VMEM((2, NX, NY, 4, NC, 8, COLS), BF16),
            pltpu.VMEM((2, ROWS, WIDTH), BF16),
            pltpu.VMEM((256, WIDTH), BF16),
            pltpu.VMEM((256, 128), F32),
            pltpu.VMEM((2, ROWS, 256), F32),
            pltpu.VMEM((8, 8, 128), F32),
            pltpu.VMEM((NZ, 8, 128), F32),
            pltpu.VMEM((8, 128), F32),
            pltpu.VMEM((16, 8, 128), F32),
            dma((8, 2)),
            dma((8, 2)),
            dma((8, NY)),
            dma((8, NY)),
            dma((NY, 8)),
            dma((NY, 8)),
            dma((NZ,)),
            dma((NZ,)),
            dma((NV,)),
            dma((NV,)),
            dma((NV,)),
            dma((NV,)),
            dma((1,)),
            dma((1,)),
            dma((NV,)),
            dma((NV,)),
            dma((NY,)),
            dma((2, NY)),
            dma((NY,)),
            dma((8,)),
            dma((8,)),
            dma((NZ,)),
            dma((8, NC)),
            dma((2, 4)),
            dma((2, 4)),
            dma((2, 4, 2)),
            dma((2, 4, 2)),
            dma((2, 4)),
            dma((2, 4)),
            dma((1,)),
            dma((1,)),
            dma((8,)),
            dma((NZ,)),
            dma((16, NC)),
            dma((16,)),
            dma((9,)),
        ],
        compiler_params=pltpu.CompilerParams(
            collective_id=0, has_side_effects=True, vmem_limit_bytes=60 * 2**20
        ),
        cost_estimate=pl.CostEstimate(
            flops=3_000_000_000, bytes_accessed=8_000_000, transcendentals=2_500_000
        ),
    )(
        span_offset,
        queries,
        cached_keys,
        cached_values,
        out_weight,
        residual,
        norm_gain,
        head_weight,
        targets,
    )
    return out[0, :8]


def solution(mesh):
    return jax.shard_map(
        body,
        mesh=mesh,
        in_specs=(
            P("seq", None),
            P(("seq", "vocab"), None),
            P(("seq", "vocab"), None),
            P("seq", "vocab"),
            P("seq", "vocab"),
            P(),
            P(("seq", "vocab"), None),
            P(),
            P(),
        ),
        out_specs=P("seq"),
        check_vma=False,
    )
```

```python
import math

import jax
import jax.numpy as jnp
from jax import lax
from jax.experimental import pallas as pl
from jax.experimental.pallas import tpu as pltpu
from jax.sharding import PartitionSpec as P

MESH = pl.DeviceIdType.MESH
HEAD_DIM = 128
NZ, NY, NX, NC = 16, 4, 4, 2
NV = NX * NC
WIDTH = 5120
COLS = WIDTH // NV
ROWS = 296
FLOOR = 1e-06
LOW = -1e30
F32 = jnp.float32
BF16 = jnp.bfloat16


def split3(x):
    hi = x.astype(BF16).astype(F32)
    rest = x - hi
    mid = rest.astype(BF16).astype(F32)
    lo = (rest - mid).astype(BF16).astype(F32)
    return hi, mid, lo


def nt(a, b, precision=None):
    return lax.dot_general(
        a, b, (((1,), (1,)), ((), ())), preferred_element_type=F32, precision=precision
    )


def kernel(
    span_ref,
    q_ref,
    k_ref,
    v_ref,
    w_ref,
    res_ref,
    gain_ref,
    head_ref,
    tgt_ref,
    out_ref,
    span_m,
    q_m,
    res_m,
    gain_m,
    tgt_m,
    gain_n,
    ginv_n,
    tgt_n,
    diff,
    q1src,
    q1buf,
    qall,
    kbuf,
    vbuf,
    wts_m,
    acc_m,
    run_m,
    osend,
    obuf,
    psrc,
    pbuf,
    att,
    abuf,
    wbuf,
    prsend,
    prbuf,
    hsend,
    hall,
    whead,
    hid_m,
    sq_m,
    logit,
    stsrc,
    stz,
    stred,
    stfin,
    kv_s,
    kv_r,
    kf_s,
    vf_s,
    kf_r,
    vf_r,
    q1_s,
    q1_r,
    qa_s,
    qa_r,
    o_s,
    o_r,
    p_s,
    p_r,
    a_s,
    a_r,
    w_s,
    w_r,
    wf_s,
    pr_s,
    pr_r,
    h_s,
    h_r,
    h1_s,
    h1_r,
    h2_s,
    h2_r,
    h3_s,
    h3_r,
    hw_s,
    hw_r,
    t1_s,
    t1_r,
    t2_s,
    t2_r,
    loc,
):
    s = lax.axis_index("seq")
    v = lax.axis_index("vocab")
    z, y, x, c = s // NY, s % NY, v // NC, v % NC
    g, par = z // 2, z % 2
    half = z // 8
    z_low = z - 8 * half
    q = y * NX + x

    def dev(zz, yy, xx, cc):
        return (zz * NY + yy, xx * NC + cc)

    def wrap(a, n):
        return jnp.where(a >= n, a - n, a)

    def flips(a):
        odd = a % 2
        return (a, a + 1 - 2 * odd, wrap(a + 2, 4), 3 - a)

    flip_x, flip_y = flips(x), flips(y)

    def push(src, dst, ss, rs, to):
        cp = pltpu.make_async_remote_copy(
            src_ref=src, dst_ref=dst, send_sem=ss, recv_sem=rs, device_id=to, device_id_type=MESH
        )
        cp.start()

    def got(ref, sem):
        pltpu.make_async_copy(ref, ref, sem).wait()

    own_head = pltpu.make_async_copy(head_ref, whead.at[0], loc.at[0])
    own_head.start()
    own_w = pltpu.make_async_copy(w_ref, wbuf.at[par, y], loc.at[1])
    own_w.start()
    own_k = pltpu.make_async_copy(
        k_ref.at[:, pl.ds(pl.multiple_of(g * 128, 128), 128)], kbuf.at[y, 0], loc.at[2]
    )
    own_k.start()
    own_v = pltpu.make_async_copy(
        v_ref.at[:, pl.ds(pl.multiple_of(g * 128, 128), 128)], vbuf.at[y, 0], loc.at[3]
    )
    own_v.start()
    loads = [
        pltpu.make_async_copy(a, b, loc.at[4 + i])
        for i, (a, b) in enumerate(
            (
                (q_ref, q_m),
                (gain_ref, gain_m),
                (tgt_ref, tgt_m),
                (span_ref, span_m),
                (res_ref, res_m),
            )
        )
    ]
    for cp in loads:
        cp.start()

    barrier = pltpu.get_barrier_semaphore()

    def greet(zz, yy, xx, cc):
        pl.semaphore_signal(barrier, inc=1, device_id=dev(zz, yy, xx, cc), device_id_type=MESH)

    @pl.loop(1, NZ)
    def _(d):
        greet(wrap(z + d, NZ), y, x, c)
        greet(wrap(z + d, NZ), y, x, 1 - c)

    greet(z, y, x, 1 - c)
    for k in range(1, 16):
        for cc in range(NC):
            greet(z, flip_y[k // 4], flip_x[k % 4], cc)

    for cp in loads:
        cp.wait()
    q_f = q_m[...].astype(F32)
    pick_row = lax.broadcasted_iota(jnp.int32, (8, 128), 0) == v
    for gg in range(8):
        rows = []
        for h in range(8 * gg, 8 * gg + 8):
            part = jnp.where(pick_row, q_f[:, h * 128 : (h + 1) * 128], 0.0)
            rows.append(jnp.sum(part, axis=0, keepdims=True))
        q1src[gg] = jnp.concatenate(rows, axis=0).astype(BF16)

    pl.semaphore_wait(barrier, 2 * (NZ - 1) + 31)

    @pl.loop(1, NZ)
    def _(d):
        to = wrap(z + d, NZ)
        push(q1src.at[to // 2], q1buf.at[z], q1_s.at[d], q1_r.at[z], dev(to, y, x, c))

    def spread(src, dst, i):
        @pl.loop(1, 8)
        def _(d):
            head = wrap(g + d, 8)
            ahead = 2 * d - par
            up = ahead <= 7
            to = dev(2 * head + jnp.where(up, 0, 1), y, x, c)
            k = jnp.where(up, ahead, 15 - ahead)
            cols = pl.ds(pl.multiple_of(head * 128, 128), 128)
            push(src.at[:, cols], dst.at[y, k], kv_s.at[d, i], kv_r.at[k, i], to)

    spread(k_ref, kbuf, 0)

    for d in range(1, NY):
        push(w_ref, wbuf.at[par, y], w_s.at[d], w_r.at[par, y], dev(z, wrap(y + d, NY), x, c))
    push(head_ref, whead.at[1], hw_s.at[0], hw_r.at[0], dev(z, y, x, 1 - c))

    gains = gain_m[...].astype(F32).reshape(WIDTH // 128, 128)
    for t in range(WIDTH // 128):
        one = gains[t : t + 1]
        lanes = slice((t % 5) * 128, (t % 5 + 1) * 128)
        gain_n[t // 5, :, lanes] = one
        ginv_n[t // 5, :, lanes] = jnp.broadcast_to(1.0 / (one * one), (8, 128))
    tgt4 = tgt_m[...].reshape(4, 128).astype(F32)
    src = lax.broadcasted_iota(jnp.int32, (128, 256), 0)
    dst = lax.broadcasted_iota(jnp.int32, (128, 256), 1)
    plane_of = lax.rem((dst // 8) % 8 + z, 8)
    here = src == (plane_of % 4) * 32 + (dst // 64) * 8 + dst % 8
    ordered = jnp.zeros((8, 256), F32)
    for r in range(2):
        row = jnp.where(c == 0, tgt4[r : r + 1], tgt4[2 + r : 3 + r])
        ordered = ordered + jnp.dot(
            jnp.broadcast_to(row, (8, 128)),
            jnp.where(here & (plane_of // 4 == r), 1.0, 0.0),
            preferred_element_type=F32,
            precision=lax.Precision.HIGHEST,
        )
    tgt_n[...] = ordered.astype(jnp.int32)

    rho = lax.broadcasted_iota(jnp.int32, (512, 512), 0)
    lane = lax.broadcasted_iota(jnp.int32, (512, 512), 1)
    slot = rho // 64
    plane_k = jnp.bitwise_and(jnp.where(par == 0, z - slot, z + slot), 15)
    pos = plane_k * 2048 + v * 64 + rho % 64
    diff[...] = pos - (32 * (2 * (lane % 8) + (lane // 64) % 2) + lane // 128)

    q1buf[z] = q1src[g]

    @pl.loop(1, NZ)
    def _(d):
        frm = wrap(z - d + NZ, NZ)
        got(q1buf.at[frm], q1_r.at[frm])

    ri = lax.broadcasted_iota(jnp.int32, (128, 128), 0)
    ci = lax.broadcasted_iota(jnp.int32, (128, 128), 1)
    from_row = (2 * (ri % 8) + ri // 64) * 8 + (ri // 8) % 8
    q_rows = q1buf[...].astype(F32).reshape(128, 128).astype(BF16)
    qall[v] = jnp.dot(
        (ci == from_row).astype(BF16), q_rows, preferred_element_type=F32
    ).astype(BF16)

    @pl.loop(1, 8)
    def _(d):
        got(kbuf.at[0, 0], kv_s.at[d, 0])

    spread(v_ref, vbuf, 1)

    @pl.loop(1, NV)
    def _(k):
        o = wrap(v + k, NV)
        push(qall.at[v], qall.at[v], qa_s.at[k], qa_r.at[v], (s, o))

    def forward(buf, i, ss, rs):
        @pl.loop(0, 8)
        def _(k):
            @pl.when(k > 0)
            def _():
                got(buf.at[y, k], kv_r.at[k, i])

            for e in (1, 3, 2):
                to = dev(z, wrap(y + e, NY), x, c)
                push(buf.at[y, k], buf.at[y, k], ss.at[k, e], rs.at[y, k], to)

    own_k.wait()
    forward(kbuf, 0, kf_s, kf_r)

    @pl.loop(1, NV)
    def _(k):
        o = wrap(v + k, NV)
        got(qall.at[o], qa_r.at[o])

    span = span_m[0]
    turn = math.log2(math.e) / math.sqrt(HEAD_DIM)

    def stat_rows(top, total):
        rows = list(split3(top)) + list(split3(total))
        return jnp.concatenate(rows + [jnp.zeros((10, top.shape[1]), F32)], axis=0).astype(BF16)

    def weigh(e):
        yy = wrap(y - e + NY, NY)
        keys = kbuf[yy].reshape(512, 128)
        for i in range(2):
            scores = nt(keys, qall[4 * i : 4 * i + 4].reshape(512, 128))
            live = diff[...] <= span + 8 * y + 4 * i - 512 * yy
            scores = jnp.where(live, scores, LOW)
            top = jnp.maximum(jnp.max(scores, axis=0, keepdims=True), 0.5 * LOW)
            wts = jnp.exp2((scores - top) * turn)
            run_m[i, e, 0:1] = top
            run_m[i, e, 1:2] = jnp.sum(wts, axis=0, keepdims=True)
            wts_m[i, e] = wts.astype(BF16)

    def mix(e):
        yy = wrap(y - e + NY, NY)
        vals_t = vbuf[yy].reshape(512, 128).T
        for i in range(2):
            tops = [run_m[i, b, 0:1] for b in range(NY)]
            top = jnp.maximum(jnp.maximum(tops[0], tops[1]), jnp.maximum(tops[2], tops[3]))
            acc = jnp.dot(vals_t, wts_m[i, e], preferred_element_type=F32)
            acc = acc * jnp.exp2((tops[e] - top) * turn)
            if e > 0:
                acc = acc + acc_m[i]
            if e < NY - 1:
                acc_m[i] = acc
                continue
            total = jnp.zeros((1, 512), F32)
            for b in range(NY):
                total = total + run_m[i, b, 1:2] * jnp.exp2((tops[b] - top) * turn)
            tail = stat_rows(top, total)
            for b in range(4):
                o = 4 * i + b
                lanes = slice(b * 128, (b + 1) * 128)
                osend[o, 0:128, :] = acc[:, lanes].astype(BF16)
                osend[o, 128:144, :] = tail[:, lanes]

                @pl.when(v != o)
                def _():
                    push(osend.at[o], obuf.at[v], o_s.at[o], o_r.at[v], (s, o))

    def arrived(e, buf, rs):
        yy = wrap(y - e + NY, NY)

        @pl.loop(0, 8)
        def _(k):
            got(buf.at[yy, k], rs.at[yy, k])

    weigh(0)
    own_v.wait()
    forward(vbuf, 1, vf_s, vf_r)
    own_w.wait()
    push(wbuf.at[par, y], wbuf.at[par, y], w_s.at[0], w_r.at[par, y], dev(z + 1 - 2 * par, y, x, c))
    for e in (1, 3, 2):
        arrived(e, kbuf, kf_r)
        weigh(e)
    mix(0)
    for e in (1, 2, 3):
        arrived(e, vbuf, vf_r)
        mix(e)

    got(wbuf.at[1 - par, y], w_r.at[1 - par, y])
    for d in range(1, NY):
        there = wbuf.at[1 - par, y]
        push(there, there, wf_s.at[d], w_r.at[1 - par, y], dev(z, wrap(y + d, NY), x, c))

    def unpack_stats(tail):
        b = tail.astype(F32)
        return b[0:1] + b[1:2] + b[2:3], b[3:4] + b[4:5] + b[5:6]

    def blend(one, two):
        m1, l1, a1 = one
        m2, l2, a2 = two
        m = jnp.maximum(m1, m2)
        f1, f2 = jnp.exp2((m1 - m) * turn), jnp.exp2((m2 - m) * turn)
        return m, l1 * f1 + l2 * f2, a1 * f1 + a2 * f2

    obuf[v] = osend[v]

    @pl.loop(1, NV)
    def _(k):
        frm = wrap(v - k + NV, NV)
        got(obuf.at[frm], o_r.at[frm])

    tails = [unpack_stats(obuf[i, 128:144, :]) for i in range(NV)]
    m_own = tails[0][0]
    for m_one, _ in tails[1:]:
        m_own = jnp.maximum(m_own, m_one)
    l_own = jnp.zeros((1, 128), F32)
    a_own = jnp.zeros((128, 128), F32)
    for i, (m_one, l_one) in enumerate(tails):
        fade = jnp.exp2((m_one - m_own) * turn)
        l_own = l_own + l_one * fade
        a_own = a_own + obuf[i, 0:128, :].astype(F32) * fade

    psrc[0:128, :] = a_own.astype(BF16)
    psrc[128:144, :] = stat_rows(m_own, l_own)
    push(psrc, pbuf, p_s.at[0], p_r.at[0], dev(z + 1 - 2 * par, y, x, c))
    got(pbuf, p_r.at[0])
    m_two, l_two = unpack_stats(pbuf[128:144, :])
    _, l_all, a_all = blend(
        (m_own, l_own, a_own), (m_two, l_two, pbuf[0:128, :].astype(F32))
    )
    att[...] = (a_all / l_all).T.astype(BF16)

    mine = att.at[pl.ds(pl.multiple_of(par * 64, 64), 64)]

    @pl.loop(1, NV)
    def _(k):
        o = wrap(v + k, NV)
        push(mine, abuf.at[v], a_s.at[k], a_r.at[v], (s, o))

    abuf[v] = att[pl.ds(pl.multiple_of(par * 64, 64), 64), :]
    for d in range(1, NY):
        frm_y = wrap(y - d + NY, NY)
        got(wbuf.at[par, frm_y], w_r.at[par, frm_y])
        got(wbuf.at[1 - par, frm_y], w_r.at[1 - par, frm_y])

    @pl.loop(1, NV)
    def _(k):
        frm = wrap(v - k + NV, NV)
        got(abuf.at[frm], a_r.at[frm])

    rows_f = abuf[...].astype(F32)
    rows = jnp.concatenate(
        [rows_f[:, h * 8 : (h + 1) * 8, :].reshape(64, 128) for h in range(8)], axis=1
    ).astype(BF16)
    proj = jnp.dot(rows, wbuf[...].reshape(1024, COLS), preferred_element_type=F32)
    r64 = lax.broadcasted_iota(jnp.int32, (64, 64), 0)
    c64 = lax.broadcasted_iota(jnp.int32, (64, 64), 1)
    to_planes = (c64 == (r64 % 8) * 8 + r64 // 8).astype(BF16)
    by_plane = jnp.dot(to_planes, proj.astype(BF16), preferred_element_type=F32)
    prsend[...] = by_plane.reshape(8, 8, COLS).astype(BF16)

    @pl.loop(1, 8)
    def _(d):
        to = wrap(g + d, 8)
        push(prsend.at[to], prbuf.at[g], pr_s.at[d], pr_r.at[g], dev(2 * to + par, y, x, c))

    hidden = res_m[...].astype(F32) + prsend[g].astype(F32)
    for d in range(1, 8):
        frm = wrap(g - d + 8, 8)
        got(prbuf.at[frm], pr_r.at[frm])
        hidden = hidden + prbuf[frm].astype(F32)
    hsend[...] = (hidden * gain_n[v]).astype(BF16)

    @pl.loop(1, NZ)
    def _(d):
        to = wrap(z + d, NZ)
        k = wrap(wrap(z_low - to + 16, 16), 8)
        slot = hall.at[k // 4, x, y, k % 4, c]
        push(hsend, slot, h_s.at[d], h_r.at[k, c], dev(to, y, x, half))

    @pl.when(c == half)
    def _():
        keep = pltpu.make_async_copy(hsend, hall.at[0, x, y, 0, c], h_r.at[0, c])
        keep.start()

    @pl.when(c != half)
    def _():
        push(hsend, hall.at[0, x, y, 0, c], h_s.at[0], h_r.at[0, c], dev(z, y, x, half))

    def piece(i, a, b):
        xx, yy = (a, b) if i == 0 else (b, a)
        return hall.at[i, xx, yy]

    def first_dev(i, d):
        return dev(z, y, wrap(x + d, NX), c) if i == 0 else dev(z, wrap(y + d, NY), x, c)

    def second_dev(i, d):
        return dev(z, wrap(y + d, NY), x, c) if i == 0 else dev(z, y, wrap(x + d, NX), c)

    def settle(i, xx, yy):
        rows = pl.ds(pl.multiple_of(yy * 64 + i * 32, 32), 32)
        squares = jnp.zeros((32, 128), F32)
        for cc in range(NC):
            hid = hall[i, xx, yy, :, cc].astype(F32).reshape(32, COLS)
            n = xx * NC + cc
            inv = ginv_n[n]
            for t in range(COLS // 128):
                part = hid[:, t * 128 : (t + 1) * 128]
                squares = squares + part * part * inv[0:1, t * 128 : (t + 1) * 128]
            cols = pl.ds(pl.multiple_of(n * COLS, 128), COLS)
            hid_m[rows, cols] = hid.astype(BF16)
        sq_m[rows, :] += squares

    def settle_line(i, b):
        @pl.loop(0, 4)
        def _(a):
            if i == 0:
                settle(i, a, b)
            else:
                settle(i, b, a)

    sq_m[...] = jnp.zeros_like(sq_m)
    lead, cross = (x, y), (y, x)
    for i in range(2):
        for k in range(4 * i, 4 * i + 4):
            for cc in range(NC):
                got(hall.at[k // 4, x, y, k % 4, cc], h_r.at[k, cc])
        for d in (1, 3, 2):
            own = piece(i, lead[i], cross[i])
            push(own, own, h1_s.at[i, d], h1_r.at[i, lead[i]], first_dev(i, d))

    def send_second(i, e, up):
        own = piece(i, wrap(lead[i] + e, 4), cross[i])
        push(own, own, h2_s.at[i, e, up], h2_r.at[i, e, up], second_dev(i, 1 if up else 3))

    for e, up in ((0, 1), (0, 0), (1, 0), (3, 1), (1, 1), (3, 0), (2, 0), (2, 1)):
        for i in range(2):
            if (e, up) in ((1, 0), (3, 1), (2, 0)):
                a = wrap(lead[i] + e, 4)
                got(piece(i, a, cross[i]), h1_r.at[i, a])
            send_second(i, e, up)

    onward = ((0, 1), (1, 0), (3, 1), (2, 0))
    for e, up in onward:
        for i in range(2):
            there = piece(i, wrap(lead[i] + e, 4), wrap(cross[i] + (3 if up else 1), 4))
            got(there, h2_r.at[i, e, up])
            push(there, there, h3_s.at[i, e], h3_r.at[i, e], second_dev(i, 1 if up else 3))

    for i in range(2):
        settle_line(i, cross[i])
    for i in range(2):
        for e, up in onward:
            there = piece(i, wrap(lead[i] + e, 4), wrap(cross[i] + (1 if up else 3), 4))
            got(there, h2_r.at[i, e, 1 - up])
        settle_line(i, wrap(cross[i] + 1, 4))
        settle_line(i, wrap(cross[i] + 3, 4))
    own_head.wait()
    got(whead.at[1], hw_r.at[0])
    for i in range(2):
        for e in range(4):
            got(piece(i, wrap(lead[i] + e, 4), wrap(cross[i] + 2, 4)), h3_r.at[i, e])
        settle_line(i, wrap(cross[i] + 2, 4))

    for p in range(2):
        logit[p] = nt(whead[p], hid_m[...])

    sums = nt(jnp.ones((8, 128), F32), sq_m[...], lax.Precision.HIGHEST)
    row_scale = lax.rsqrt(sums[0:1] / WIDTH + FLOOR)
    targets = tgt_n[0:1]
    row_id = lax.broadcasted_iota(jnp.int32, (ROWS, 256), 0)
    tops, parts, picks = [], [], []
    for p in range(2):
        block = s * NV + (v if p == 0 else v + 1 - 2 * c)
        lg = logit[p] * row_scale
        logit[p] = lg
        picks.append(
            jnp.sum(jnp.where(row_id == targets - block * ROWS, lg, 0.0), axis=0, keepdims=True)
        )
        tops.append(jnp.max(lg, axis=0, keepdims=True))
    top = jnp.maximum(tops[0], tops[1])
    for p in range(2):
        parts.append(jnp.sum(jnp.exp(logit[p] - top), axis=0, keepdims=True))
    stats = jnp.concatenate(
        [top, parts[0] + parts[1], picks[0] + picks[1], jnp.zeros((5, 256), F32)], axis=0
    )
    stsrc[...] = jnp.zeros_like(stsrc)
    for k in range(8):
        for yy in range(NY):
            first = yy * 64 + k * 8
            stsrc[k, :, yy * 8 : (yy + 1) * 8] = stats[:, first : first + 8]

    def join_all(ref, n):
        m = ref[0, 0:1]
        for i in range(1, n):
            m = jnp.maximum(m, ref[i, 0:1])
        t = jnp.zeros_like(m)
        picked = jnp.zeros_like(m)
        for i in range(n):
            t = t + ref[i, 1:2] * jnp.exp(ref[i, 0:1] - m)
            picked = picked + ref[i, 2:3]
        return m, t, picked

    @pl.loop(0, 8)
    def _(k):
        to = 8 * c + wrap(z_low + k, 8)

        @pl.when(to != z)
        def _():
            push(stsrc.at[k], stz.at[z], t1_s.at[k], t1_r.at[z], dev(to, y, x, c))

    @pl.when(c == half)
    def _():
        stz[z] = stsrc[0]

        @pl.loop(1, NZ)
        def _(d):
            frm = wrap(z + d, NZ)
            got(stz.at[frm], t1_r.at[frm])

        m, t, picked = join_all(stz, NZ)
        stred[...] = jnp.concatenate([m, t, picked, jnp.zeros((5, 128), F32)], axis=0)

        push(stred, stfin.at[q], t2_s.at[0, 0], t2_r.at[q], dev(z, y, x, 1 - c))
        for k in (1, 4, 3, 12, 2, 8, 5, 15, 6, 9, 7, 13, 10, 11, 14):
            for cc in range(NC):
                to = dev(z, flip_y[k // 4], flip_x[k % 4], cc)
                push(stred, stfin.at[q], t2_s.at[k, cc], t2_r.at[q], to)
        stfin[q] = stred[...]

    @pl.when(c != half)
    def _():
        got(stfin.at[q], t2_r.at[q])

    for k in range(1, 16):
        o = flip_y[k // 4] * NX + flip_x[k % 4]
        got(stfin.at[o], t2_r.at[o])

    m, t, picked = join_all(stfin, 16)
    logprob = picked - m - jnp.log(t)
    shift = lax.rem(128 - y * 8, 128)
    out_ref[...] = pltpu.roll(jnp.broadcast_to(logprob, (8, 128)), shift, 1)

    @pl.loop(1, NZ)
    def _(d):
        got(q1src.at[0], q1_s.at[d])
        got(hsend, h_s.at[d])

    @pl.when(c != half)
    def _():
        got(hsend, h_s.at[0])

    @pl.loop(1, 8)
    def _(d):
        got(vbuf.at[0, 0], kv_s.at[d, 1])
        got(qall.at[0], qa_s.at[d])
        got(prsend.at[0], pr_s.at[d])
        got(abuf.at[0], a_s.at[d])

    @pl.loop(0, NV)
    def _(o):
        @pl.when(o != v)
        def _():
            got(osend.at[0], o_s.at[o])

    got(wbuf.at[0, 0], w_s.at[0])
    for d in range(1, NY):
        got(wbuf.at[0, 0], w_s.at[d])
        got(wbuf.at[0, 0], wf_s.at[d])

        @pl.loop(0, 8)
        def _(k):
            got(kbuf.at[0, 0], kf_s.at[k, d])
            got(vbuf.at[0, 0], vf_s.at[k, d])

    got(whead.at[1], hw_s.at[0])
    got(psrc, p_s.at[0])

    for i in range(2):
        for d in range(1, 4):
            got(piece(i, 0, 0), h1_s.at[i, d])
        for a in range(4):
            got(piece(i, 0, 0), h2_s.at[i, a, 0])
            got(piece(i, 0, 0), h2_s.at[i, a, 1])
            got(piece(i, 0, 0), h3_s.at[i, a])

    @pl.loop(0, 8)
    def _(k):
        @pl.when(8 * c + wrap(z_low + k, 8) != z)
        def _():
            got(stsrc.at[0], t1_s.at[k])

    @pl.when(c == half)
    def _():
        got(stred, t2_s.at[0, 0])

        @pl.loop(1, 16)
        def _(k):
            for cc in range(NC):
                got(stred, t2_s.at[k, cc])


def body(
    queries,
    cached_keys,
    cached_values,
    out_weight,
    residual,
    norm_gain,
    head_weight,
    targets,
    span_offset,
):
    vm = pl.BlockSpec(memory_space=pltpu.VMEM)
    hbm = pl.BlockSpec(memory_space=pl.ANY)
    dma = pltpu.SemaphoreType.DMA
    out = pl.pallas_call(
        kernel,
        out_shape=jax.ShapeDtypeStruct((8, 128), F32),
        in_specs=[hbm] * 9,
        out_specs=vm,
        scratch_shapes=[
            pltpu.SMEM((1,), jnp.int32),
            pltpu.VMEM((8, 64 * HEAD_DIM), BF16),
            pltpu.VMEM((8, COLS), BF16),
            pltpu.VMEM((WIDTH,), BF16),
            pltpu.VMEM((512,), jnp.int32),
            pltpu.VMEM((NV, 1, COLS), F32),
            pltpu.VMEM((NV, 8, COLS), F32),
            pltpu.VMEM((8, 256), jnp.int32),
            pltpu.VMEM((512, 512), jnp.int32),
            pltpu.VMEM((8, 8, 128), BF16),
            pltpu.VMEM((NZ, 8, 128), BF16),
            pltpu.VMEM((NV, 128, 128), BF16),
            pltpu.VMEM((NY, 8, 64, 128), BF16),
            pltpu.VMEM((NY, 8, 64, 128), BF16),
            pltpu.VMEM((2, NY, 512, 512), BF16),
            pltpu.VMEM((2, 128, 512), F32),
            pltpu.VMEM((2, NY, 8, 512), F32),
            pltpu.VMEM((NV, 144, 128), BF16),
            pltpu.VMEM((NV, 144, 128), BF16),
            pltpu.VMEM((144, 128), BF16),
            pltpu.VMEM((144, 128), BF16),
            pltpu.VMEM((128, 128), BF16),
            pltpu.VMEM((NV, 64, 128), BF16),
            pltpu.VMEM((2, NY, 128, COLS), BF16),
            pltpu.VMEM((8, 8, COLS), BF16),
            pltpu.VMEM((8, 8, COLS), BF16),
            pltpu.VMEM((8, COLS), BF16),
            pltpu.VMEM((2, NX, NY, 4, NC, 8, COLS), BF16),
            pltpu.VMEM((2, ROWS, WIDTH), BF16),
            pltpu.VMEM((256, WIDTH), BF16),
            pltpu.VMEM((256, 128), F32),
            pltpu.VMEM((2, ROWS, 256), F32),
            pltpu.VMEM((8, 8, 128), F32),
            pltpu.VMEM((NZ, 8, 128), F32),
            pltpu.VMEM((8, 128), F32),
            pltpu.VMEM((16, 8, 128), F32),
            dma((8, 2)),
            dma((8, 2)),
            dma((8, NY)),
            dma((8, NY)),
            dma((NY, 8)),
            dma((NY, 8)),
            dma((NZ,)),
            dma((NZ,)),
            dma((NV,)),
            dma((NV,)),
            dma((NV,)),
            dma((NV,)),
            dma((1,)),
            dma((1,)),
            dma((NV,)),
            dma((NV,)),
            dma((NY,)),
            dma((2, NY)),
            dma((NY,)),
            dma((8,)),
            dma((8,)),
            dma((NZ,)),
            dma((8, NC)),
            dma((2, 4)),
            dma((2, 4)),
            dma((2, 4, 2)),
            dma((2, 4, 2)),
            dma((2, 4)),
            dma((2, 4)),
            dma((1,)),
            dma((1,)),
            dma((8,)),
            dma((NZ,)),
            dma((16, NC)),
            dma((16,)),
            dma((9,)),
        ],
        compiler_params=pltpu.CompilerParams(
            collective_id=0, has_side_effects=True, vmem_limit_bytes=60 * 2**20
        ),
        cost_estimate=pl.CostEstimate(
            flops=3_000_000_000, bytes_accessed=8_000_000, transcendentals=2_500_000
        ),
    )(
        span_offset,
        queries,
        cached_keys,
        cached_values,
        out_weight,
        residual,
        norm_gain,
        head_weight,
        targets,
    )
    return out[0, :8]


def solution(mesh):
    return jax.shard_map(
        body,
        mesh=mesh,
        in_specs=(
            P("seq", None),
            P(("seq", "vocab"), None),
            P(("seq", "vocab"), None),
            P("seq", "vocab"),
            P("seq", "vocab"),
            P(),
            P(("seq", "vocab"), None),
            P(),
            P(),
        ),
        out_specs=P("seq"),
        check_vma=False,
    )
```

```python
import math

import jax
import jax.numpy as jnp
from jax import lax
from jax.experimental import pallas as pl
from jax.experimental.pallas import tpu as pltpu
from jax.sharding import PartitionSpec as P

MESH = pl.DeviceIdType.MESH
HEAD_DIM = 128
NZ, NY, NX, NC = 16, 4, 4, 2
NV = NX * NC
WIDTH = 5120
COLS = WIDTH // NV
ROWS = 296
FLOOR = 1e-06
LOW = -1e30
F32 = jnp.float32
BF16 = jnp.bfloat16


def split3(x):
    hi = x.astype(BF16).astype(F32)
    rest = x - hi
    mid = rest.astype(BF16).astype(F32)
    lo = (rest - mid).astype(BF16).astype(F32)
    return hi, mid, lo


def nt(a, b, precision=None):
    return lax.dot_general(
        a, b, (((1,), (1,)), ((), ())), preferred_element_type=F32, precision=precision
    )


def kernel(
    span_ref,
    q_ref,
    k_ref,
    v_ref,
    w_ref,
    res_ref,
    gain_ref,
    head_ref,
    tgt_ref,
    out_ref,
    span_m,
    q_m,
    res_m,
    gain_m,
    tgt_m,
    gain_n,
    ginv_n,
    tgt_n,
    diff,
    q1src,
    q1buf,
    qall,
    kbuf,
    vbuf,
    wts_m,
    acc_m,
    run_m,
    osend,
    obuf,
    psrc,
    pbuf,
    att,
    abuf,
    wbuf,
    prsend,
    prbuf,
    hsend,
    hall,
    whead,
    hid_m,
    sq_m,
    logit,
    stsrc,
    stz,
    stred,
    stfin,
    kv_s,
    kv_r,
    kf_s,
    vf_s,
    kf_r,
    vf_r,
    q1_s,
    q1_r,
    qa_s,
    qa_r,
    o_s,
    o_r,
    p_s,
    p_r,
    a_s,
    a_r,
    w_s,
    w_r,
    wf_s,
    pr_s,
    pr_r,
    h_s,
    h_r,
    h1_s,
    h1_r,
    h2_s,
    h2_r,
    h3_s,
    h3_r,
    hw_s,
    hw_r,
    t1_s,
    t1_r,
    t2_s,
    t2_r,
    loc,
):
    s = lax.axis_index("seq")
    v = lax.axis_index("vocab")
    z, y, x, c = s // NY, s % NY, v // NC, v % NC
    g, par = z // 2, z % 2
    half = z // 8
    z_low = z - 8 * half
    q = y * NX + x

    def dev(zz, yy, xx, cc):
        return (zz * NY + yy, xx * NC + cc)

    def wrap(a, n):
        return jnp.where(a >= n, a - n, a)

    def flips(a):
        odd = a % 2
        return (a, a + 1 - 2 * odd, wrap(a + 2, 4), 3 - a)

    flip_x, flip_y = flips(x), flips(y)

    def push(src, dst, ss, rs, to):
        cp = pltpu.make_async_remote_copy(
            src_ref=src, dst_ref=dst, send_sem=ss, recv_sem=rs, device_id=to, device_id_type=MESH
        )
        cp.start()

    def got(ref, sem):
        pltpu.make_async_copy(ref, ref, sem).wait()

    own_head = pltpu.make_async_copy(head_ref, whead.at[0], loc.at[0])
    own_head.start()
    own_w = pltpu.make_async_copy(w_ref, wbuf.at[par, y], loc.at[1])
    own_w.start()
    own_k = pltpu.make_async_copy(
        k_ref.at[:, pl.ds(pl.multiple_of(g * 128, 128), 128)], kbuf.at[y, 0], loc.at[2]
    )
    own_k.start()
    own_v = pltpu.make_async_copy(
        v_ref.at[:, pl.ds(pl.multiple_of(g * 128, 128), 128)], vbuf.at[y, 0], loc.at[3]
    )
    own_v.start()
    loads = [
        pltpu.make_async_copy(a, b, loc.at[4 + i])
        for i, (a, b) in enumerate(
            (
                (q_ref, q_m),
                (gain_ref, gain_m),
                (tgt_ref, tgt_m),
                (span_ref, span_m),
                (res_ref, res_m),
            )
        )
    ]
    for cp in loads:
        cp.start()

    barrier = pltpu.get_barrier_semaphore()

    def greet(zz, yy, xx, cc):
        pl.semaphore_signal(barrier, inc=1, device_id=dev(zz, yy, xx, cc), device_id_type=MESH)

    @pl.loop(1, NZ)
    def _(d):
        greet(wrap(z + d, NZ), y, x, c)
        greet(wrap(z + d, NZ), y, x, 1 - c)

    greet(z, y, x, 1 - c)
    for k in range(1, 16):
        for cc in range(NC):
            greet(z, flip_y[k // 4], flip_x[k % 4], cc)

    for cp in loads:
        cp.wait()
    q_f = q_m[...].astype(F32)
    pick_row = lax.broadcasted_iota(jnp.int32, (8, 128), 0) == v
    for gg in range(8):
        rows = []
        for h in range(8 * gg, 8 * gg + 8):
            part = jnp.where(pick_row, q_f[:, h * 128 : (h + 1) * 128], 0.0)
            rows.append(jnp.sum(part, axis=0, keepdims=True))
        q1src[gg] = jnp.concatenate(rows, axis=0).astype(BF16)

    pl.semaphore_wait(barrier, 2 * (NZ - 1) + 31)

    def spread(src, dst, i):
        @pl.loop(1, 8)
        def _(d):
            head = wrap(g + d, 8)
            ahead = 2 * d - par
            up = ahead <= 7
            to = dev(2 * head + jnp.where(up, 0, 1), y, x, c)
            k = jnp.where(up, ahead, 15 - ahead)
            cols = pl.ds(pl.multiple_of(head * 128, 128), 128)
            push(src.at[:, cols], dst.at[y, k], kv_s.at[d, i], kv_r.at[k, i], to)

    spread(k_ref, kbuf, 0)

    @pl.loop(1, NZ)
    def _(d):
        to = wrap(z + d, NZ)
        push(q1src.at[to // 2], q1buf.at[z], q1_s.at[d], q1_r.at[z], dev(to, y, x, c))

    for d in range(1, NY):
        push(w_ref, wbuf.at[par, y], w_s.at[d], w_r.at[par, y], dev(z, wrap(y + d, NY), x, c))
    push(head_ref, whead.at[1], hw_s.at[0], hw_r.at[0], dev(z, y, x, 1 - c))

    gains = gain_m[...].astype(F32).reshape(WIDTH // 128, 128)
    for t in range(WIDTH // 128):
        one = gains[t : t + 1]
        lanes = slice((t % 5) * 128, (t % 5 + 1) * 128)
        gain_n[t // 5, :, lanes] = one
        ginv_n[t // 5, :, lanes] = jnp.broadcast_to(1.0 / (one * one), (8, 128))
    tgt4 = tgt_m[...].reshape(4, 128).astype(F32)
    src = lax.broadcasted_iota(jnp.int32, (128, 256), 0)
    dst = lax.broadcasted_iota(jnp.int32, (128, 256), 1)
    plane_of = lax.rem((dst // 8) % 8 + z, 8)
    here = src == (plane_of % 4) * 32 + (dst // 64) * 8 + dst % 8
    ordered = jnp.zeros((8, 256), F32)
    for r in range(2):
        row = jnp.where(c == 0, tgt4[r : r + 1], tgt4[2 + r : 3 + r])
        ordered = ordered + jnp.dot(
            jnp.broadcast_to(row, (8, 128)),
            jnp.where(here & (plane_of // 4 == r), 1.0, 0.0),
            preferred_element_type=F32,
            precision=lax.Precision.HIGHEST,
        )
    tgt_n[...] = ordered.astype(jnp.int32)

    rho = lax.broadcasted_iota(jnp.int32, (512, 512), 0)
    lane = lax.broadcasted_iota(jnp.int32, (512, 512), 1)
    slot = rho // 64
    plane_k = jnp.bitwise_and(jnp.where(par == 0, z - slot, z + slot), 15)
    pos = plane_k * 2048 + v * 64 + rho % 64
    diff[...] = pos - (32 * (2 * (lane % 8) + (lane // 64) % 2) + lane // 128)

    q1buf[z] = q1src[g]

    @pl.loop(1, NZ)
    def _(d):
        frm = wrap(z - d + NZ, NZ)
        got(q1buf.at[frm], q1_r.at[frm])

    ri = lax.broadcasted_iota(jnp.int32, (128, 128), 0)
    ci = lax.broadcasted_iota(jnp.int32, (128, 128), 1)
    from_row = (2 * (ri % 8) + ri // 64) * 8 + (ri // 8) % 8
    q_rows = q1buf[...].astype(F32).reshape(128, 128).astype(BF16)
    qall[v] = jnp.dot(
        (ci == from_row).astype(BF16), q_rows, preferred_element_type=F32
    ).astype(BF16)

    @pl.loop(1, 8)
    def _(d):
        got(kbuf.at[0, 0], kv_s.at[d, 0])

    spread(v_ref, vbuf, 1)

    @pl.loop(1, NV)
    def _(k):
        o = wrap(v + k, NV)
        push(qall.at[v], qall.at[v], qa_s.at[k], qa_r.at[v], (s, o))

    def forward(buf, i, ss, rs):
        @pl.loop(0, 8)
        def _(k):
            @pl.when(k > 0)
            def _():
                got(buf.at[y, k], kv_r.at[k, i])

            for e in (1, 3, 2):
                to = dev(z, wrap(y + e, NY), x, c)
                push(buf.at[y, k], buf.at[y, k], ss.at[k, e], rs.at[y, k], to)

    own_k.wait()
    forward(kbuf, 0, kf_s, kf_r)

    @pl.loop(1, NV)
    def _(k):
        o = wrap(v + k, NV)
        got(qall.at[o], qa_r.at[o])

    span = span_m[0]
    turn = math.log2(math.e) / math.sqrt(HEAD_DIM)

    def stat_rows(top, total):
        rows = list(split3(top)) + list(split3(total))
        return jnp.concatenate(rows + [jnp.zeros((10, top.shape[1]), F32)], axis=0).astype(BF16)

    def weigh(e):
        yy = wrap(y - e + NY, NY)
        keys = kbuf[yy].reshape(512, 128)
        for i in range(2):
            scores = nt(keys, qall[4 * i : 4 * i + 4].reshape(512, 128))
            live = diff[...] <= span + 8 * y + 4 * i - 512 * yy
            scores = jnp.where(live, scores, LOW)
            top = jnp.maximum(jnp.max(scores, axis=0, keepdims=True), 0.5 * LOW)
            wts = jnp.exp2((scores - top) * turn)
            run_m[i, e, 0:1] = top
            run_m[i, e, 1:2] = jnp.sum(wts, axis=0, keepdims=True)
            wts_m[i, e] = wts.astype(BF16)

    def mix(e):
        yy = wrap(y - e + NY, NY)
        vals_t = vbuf[yy].reshape(512, 128).T
        for i in range(2):
            tops = [run_m[i, b, 0:1] for b in range(NY)]
            top = jnp.maximum(jnp.maximum(tops[0], tops[1]), jnp.maximum(tops[2], tops[3]))
            acc = jnp.dot(vals_t, wts_m[i, e], preferred_element_type=F32)
            acc = acc * jnp.exp2((tops[e] - top) * turn)
            if e > 0:
                acc = acc + acc_m[i]
            if e < NY - 1:
                acc_m[i] = acc
                continue
            total = jnp.zeros((1, 512), F32)
            for b in range(NY):
                total = total + run_m[i, b, 1:2] * jnp.exp2((tops[b] - top) * turn)
            tail = stat_rows(top, total)
            for b in range(4):
                o = 4 * i + b
                lanes = slice(b * 128, (b + 1) * 128)
                osend[o, 0:128, :] = acc[:, lanes].astype(BF16)
                osend[o, 128:144, :] = tail[:, lanes]

                @pl.when(v != o)
                def _():
                    push(osend.at[o], obuf.at[v], o_s.at[o], o_r.at[v], (s, o))

    def arrived(e, buf, rs):
        yy = wrap(y - e + NY, NY)

        @pl.loop(0, 8)
        def _(k):
            got(buf.at[yy, k], rs.at[yy, k])

    weigh(0)
    own_v.wait()
    forward(vbuf, 1, vf_s, vf_r)
    own_w.wait()
    push(wbuf.at[par, y], wbuf.at[par, y], w_s.at[0], w_r.at[par, y], dev(z + 1 - 2 * par, y, x, c))
    for e in (1, 3, 2):
        arrived(e, kbuf, kf_r)
        weigh(e)
    mix(0)
    for e in (1, 2, 3):
        arrived(e, vbuf, vf_r)
        mix(e)

    got(wbuf.at[1 - par, y], w_r.at[1 - par, y])
    for d in range(1, NY):
        there = wbuf.at[1 - par, y]
        push(there, there, wf_s.at[d], w_r.at[1 - par, y], dev(z, wrap(y + d, NY), x, c))

    def unpack_stats(tail):
        b = tail.astype(F32)
        return b[0:1] + b[1:2] + b[2:3], b[3:4] + b[4:5] + b[5:6]

    def blend(one, two):
        m1, l1, a1 = one
        m2, l2, a2 = two
        m = jnp.maximum(m1, m2)
        f1, f2 = jnp.exp2((m1 - m) * turn), jnp.exp2((m2 - m) * turn)
        return m, l1 * f1 + l2 * f2, a1 * f1 + a2 * f2

    obuf[v] = osend[v]

    @pl.loop(1, NV)
    def _(k):
        frm = wrap(v - k + NV, NV)
        got(obuf.at[frm], o_r.at[frm])

    tails = [unpack_stats(obuf[i, 128:144, :]) for i in range(NV)]
    m_own = tails[0][0]
    for m_one, _ in tails[1:]:
        m_own = jnp.maximum(m_own, m_one)
    l_own = jnp.zeros((1, 128), F32)
    a_own = jnp.zeros((128, 128), F32)
    for i, (m_one, l_one) in enumerate(tails):
        fade = jnp.exp2((m_one - m_own) * turn)
        l_own = l_own + l_one * fade
        a_own = a_own + obuf[i, 0:128, :].astype(F32) * fade

    psrc[0:128, :] = a_own.astype(BF16)
    psrc[128:144, :] = stat_rows(m_own, l_own)
    push(psrc, pbuf, p_s.at[0], p_r.at[0], dev(z + 1 - 2 * par, y, x, c))
    got(pbuf, p_r.at[0])
    m_two, l_two = unpack_stats(pbuf[128:144, :])
    _, l_all, a_all = blend(
        (m_own, l_own, a_own), (m_two, l_two, pbuf[0:128, :].astype(F32))
    )
    att[...] = (a_all / l_all).T.astype(BF16)

    mine = att.at[pl.ds(pl.multiple_of(par * 64, 64), 64)]

    @pl.loop(1, NV)
    def _(k):
        o = wrap(v + k, NV)
        push(mine, abuf.at[v], a_s.at[k], a_r.at[v], (s, o))

    abuf[v] = att[pl.ds(pl.multiple_of(par * 64, 64), 64), :]
    for d in range(1, NY):
        frm_y = wrap(y - d + NY, NY)
        got(wbuf.at[par, frm_y], w_r.at[par, frm_y])
        got(wbuf.at[1 - par, frm_y], w_r.at[1 - par, frm_y])

    @pl.loop(1, NV)
    def _(k):
        frm = wrap(v - k + NV, NV)
        got(abuf.at[frm], a_r.at[frm])

    rows_f = abuf[...].astype(F32)
    rows = jnp.concatenate(
        [rows_f[:, h * 8 : (h + 1) * 8, :].reshape(64, 128) for h in range(8)], axis=1
    ).astype(BF16)
    proj = jnp.dot(rows, wbuf[...].reshape(1024, COLS), preferred_element_type=F32)
    r64 = lax.broadcasted_iota(jnp.int32, (64, 64), 0)
    c64 = lax.broadcasted_iota(jnp.int32, (64, 64), 1)
    to_planes = (c64 == (r64 % 8) * 8 + r64 // 8).astype(BF16)
    by_plane = jnp.dot(to_planes, proj.astype(BF16), preferred_element_type=F32)
    prsend[...] = by_plane.reshape(8, 8, COLS).astype(BF16)

    @pl.loop(1, 8)
    def _(i):
        d = jnp.where(i % 2 == 1, (i + 1) // 2, 8 - i // 2)
        to = wrap(g + d, 8)
        push(prsend.at[to], prbuf.at[g], pr_s.at[d], pr_r.at[g], dev(2 * to + par, y, x, c))

    hidden = res_m[...].astype(F32) + prsend[g].astype(F32)
    for d in range(1, 8):
        frm = wrap(g - d + 8, 8)
        got(prbuf.at[frm], pr_r.at[frm])
        hidden = hidden + prbuf[frm].astype(F32)
    hsend[...] = (hidden * gain_n[v]).astype(BF16)

    @pl.loop(1, NZ)
    def _(i):
        d = jnp.where(i % 2 == 1, (i + 1) // 2, NZ - i // 2)
        to = wrap(z + d, NZ)
        k = wrap(wrap(z_low - to + 16, 16), 8)
        slot = hall.at[k // 4, x, y, k % 4, c]
        push(hsend, slot, h_s.at[d], h_r.at[k, c], dev(to, y, x, half))

    @pl.when(c == half)
    def _():
        keep = pltpu.make_async_copy(hsend, hall.at[0, x, y, 0, c], h_r.at[0, c])
        keep.start()

    @pl.when(c != half)
    def _():
        push(hsend, hall.at[0, x, y, 0, c], h_s.at[0], h_r.at[0, c], dev(z, y, x, half))

    def piece(i, a, b):
        xx, yy = (a, b) if i == 0 else (b, a)
        return hall.at[i, xx, yy]

    def first_dev(i, d):
        return dev(z, y, wrap(x + d, NX), c) if i == 0 else dev(z, wrap(y + d, NY), x, c)

    def second_dev(i, d):
        return dev(z, wrap(y + d, NY), x, c) if i == 0 else dev(z, y, wrap(x + d, NX), c)

    def settle(i, xx, yy):
        rows = pl.ds(pl.multiple_of(yy * 64 + i * 32, 32), 32)
        squares = jnp.zeros((32, 128), F32)
        for cc in range(NC):
            hid = hall[i, xx, yy, :, cc].astype(F32).reshape(32, COLS)
            n = xx * NC + cc
            inv = ginv_n[n]
            for t in range(COLS // 128):
                part = hid[:, t * 128 : (t + 1) * 128]
                squares = squares + part * part * inv[0:1, t * 128 : (t + 1) * 128]
            cols = pl.ds(pl.multiple_of(n * COLS, 128), COLS)
            hid_m[rows, cols] = hid.astype(BF16)
        sq_m[rows, :] += squares

    def settle_line(i, b):
        @pl.loop(0, 4)
        def _(a):
            if i == 0:
                settle(i, a, b)
            else:
                settle(i, b, a)

    sq_m[...] = jnp.zeros_like(sq_m)
    lead, cross = (x, y), (y, x)
    for i in range(2):
        for k in range(4 * i, 4 * i + 4):
            for cc in range(NC):
                got(hall.at[k // 4, x, y, k % 4, cc], h_r.at[k, cc])
        for d in (1, 3, 2):
            own = piece(i, lead[i], cross[i])
            push(own, own, h1_s.at[i, d], h1_r.at[i, lead[i]], first_dev(i, d))

    def send_second(i, e, up):
        own = piece(i, wrap(lead[i] + e, 4), cross[i])
        push(own, own, h2_s.at[i, e, up], h2_r.at[i, e, up], second_dev(i, 1 if up else 3))

    for e, up in ((0, 1), (0, 0), (1, 0), (3, 1), (1, 1), (3, 0), (2, 0), (2, 1)):
        for i in range(2):
            if (e, up) in ((1, 0), (3, 1), (2, 0)):
                a = wrap(lead[i] + e, 4)
                got(piece(i, a, cross[i]), h1_r.at[i, a])
            send_second(i, e, up)

    onward = ((0, 1), (1, 0), (3, 1), (2, 0))
    for e, up in onward:
        for i in range(2):
            there = piece(i, wrap(lead[i] + e, 4), wrap(cross[i] + (3 if up else 1), 4))
            got(there, h2_r.at[i, e, up])
            push(there, there, h3_s.at[i, e], h3_r.at[i, e], second_dev(i, 1 if up else 3))

    for i in range(2):
        settle_line(i, cross[i])
    for i in range(2):
        for e, up in onward:
            there = piece(i, wrap(lead[i] + e, 4), wrap(cross[i] + (1 if up else 3), 4))
            got(there, h2_r.at[i, e, 1 - up])
        settle_line(i, wrap(cross[i] + 1, 4))
        settle_line(i, wrap(cross[i] + 3, 4))
    own_head.wait()
    got(whead.at[1], hw_r.at[0])
    for i in range(2):
        for e in range(4):
            got(piece(i, wrap(lead[i] + e, 4), wrap(cross[i] + 2, 4)), h3_r.at[i, e])
        settle_line(i, wrap(cross[i] + 2, 4))

    for p in range(2):
        logit[p] = nt(whead[p], hid_m[...])

    sums = nt(jnp.ones((8, 128), F32), sq_m[...], lax.Precision.HIGHEST)
    row_scale = lax.rsqrt(sums[0:1] / WIDTH + FLOOR)
    targets = tgt_n[0:1]
    row_id = lax.broadcasted_iota(jnp.int32, (ROWS, 256), 0)
    tops, parts, picks = [], [], []
    for p in range(2):
        block = s * NV + (v if p == 0 else v + 1 - 2 * c)
        lg = logit[p] * row_scale
        logit[p] = lg
        picks.append(
            jnp.sum(jnp.where(row_id == targets - block * ROWS, lg, 0.0), axis=0, keepdims=True)
        )
        tops.append(jnp.max(lg, axis=0, keepdims=True))
    top = jnp.maximum(tops[0], tops[1])
    for p in range(2):
        parts.append(jnp.sum(jnp.exp(logit[p] - top), axis=0, keepdims=True))
    stats = jnp.concatenate(
        [top, parts[0] + parts[1], picks[0] + picks[1], jnp.zeros((5, 256), F32)], axis=0
    )
    stsrc[...] = jnp.zeros_like(stsrc)
    for k in range(8):
        for yy in range(NY):
            first = yy * 64 + k * 8
            stsrc[k, :, yy * 8 : (yy + 1) * 8] = stats[:, first : first + 8]

    def join_all(ref, n):
        m = ref[0, 0:1]
        for i in range(1, n):
            m = jnp.maximum(m, ref[i, 0:1])
        t = jnp.zeros_like(m)
        picked = jnp.zeros_like(m)
        for i in range(n):
            t = t + ref[i, 1:2] * jnp.exp(ref[i, 0:1] - m)
            picked = picked + ref[i, 2:3]
        return m, t, picked

    @pl.loop(0, 8)
    def _(k):
        to = 8 * c + wrap(z_low + k, 8)

        @pl.when(to != z)
        def _():
            push(stsrc.at[k], stz.at[z], t1_s.at[k], t1_r.at[z], dev(to, y, x, c))

    @pl.when(c == half)
    def _():
        stz[z] = stsrc[0]

        @pl.loop(1, NZ)
        def _(d):
            frm = wrap(z + d, NZ)
            got(stz.at[frm], t1_r.at[frm])

        m, t, picked = join_all(stz, NZ)
        stred[...] = jnp.concatenate([m, t, picked, jnp.zeros((5, 128), F32)], axis=0)

        push(stred, stfin.at[q], t2_s.at[0, 0], t2_r.at[q], dev(z, y, x, 1 - c))
        for k in (1, 4, 3, 12, 2, 8, 5, 15, 6, 9, 7, 13, 10, 11, 14):
            for cc in range(NC):
                to = dev(z, flip_y[k // 4], flip_x[k % 4], cc)
                push(stred, stfin.at[q], t2_s.at[k, cc], t2_r.at[q], to)
        stfin[q] = stred[...]

    @pl.when(c != half)
    def _():
        got(stfin.at[q], t2_r.at[q])

    for k in range(1, 16):
        o = flip_y[k // 4] * NX + flip_x[k % 4]
        got(stfin.at[o], t2_r.at[o])

    m, t, picked = join_all(stfin, 16)
    logprob = picked - m - jnp.log(t)
    shift = lax.rem(128 - y * 8, 128)
    out_ref[...] = pltpu.roll(jnp.broadcast_to(logprob, (8, 128)), shift, 1)

    @pl.loop(1, NZ)
    def _(d):
        got(q1src.at[0], q1_s.at[d])
        got(hsend, h_s.at[d])

    @pl.when(c != half)
    def _():
        got(hsend, h_s.at[0])

    @pl.loop(1, 8)
    def _(d):
        got(vbuf.at[0, 0], kv_s.at[d, 1])
        got(qall.at[0], qa_s.at[d])
        got(prsend.at[0], pr_s.at[d])
        got(abuf.at[0], a_s.at[d])

    @pl.loop(0, NV)
    def _(o):
        @pl.when(o != v)
        def _():
            got(osend.at[0], o_s.at[o])

    got(wbuf.at[0, 0], w_s.at[0])
    for d in range(1, NY):
        got(wbuf.at[0, 0], w_s.at[d])
        got(wbuf.at[0, 0], wf_s.at[d])

        @pl.loop(0, 8)
        def _(k):
            got(kbuf.at[0, 0], kf_s.at[k, d])
            got(vbuf.at[0, 0], vf_s.at[k, d])

    got(whead.at[1], hw_s.at[0])
    got(psrc, p_s.at[0])

    for i in range(2):
        for d in range(1, 4):
            got(piece(i, 0, 0), h1_s.at[i, d])
        for a in range(4):
            got(piece(i, 0, 0), h2_s.at[i, a, 0])
            got(piece(i, 0, 0), h2_s.at[i, a, 1])
            got(piece(i, 0, 0), h3_s.at[i, a])

    @pl.loop(0, 8)
    def _(k):
        @pl.when(8 * c + wrap(z_low + k, 8) != z)
        def _():
            got(stsrc.at[0], t1_s.at[k])

    @pl.when(c == half)
    def _():
        got(stred, t2_s.at[0, 0])

        @pl.loop(1, 16)
        def _(k):
            for cc in range(NC):
                got(stred, t2_s.at[k, cc])


def body(
    queries,
    cached_keys,
    cached_values,
    out_weight,
    residual,
    norm_gain,
    head_weight,
    targets,
    span_offset,
):
    vm = pl.BlockSpec(memory_space=pltpu.VMEM)
    hbm = pl.BlockSpec(memory_space=pl.ANY)
    dma = pltpu.SemaphoreType.DMA
    out = pl.pallas_call(
        kernel,
        out_shape=jax.ShapeDtypeStruct((8, 128), F32),
        in_specs=[hbm] * 9,
        out_specs=vm,
        scratch_shapes=[
            pltpu.SMEM((1,), jnp.int32),
            pltpu.VMEM((8, 64 * HEAD_DIM), BF16),
            pltpu.VMEM((8, COLS), BF16),
            pltpu.VMEM((WIDTH,), BF16),
            pltpu.VMEM((512,), jnp.int32),
            pltpu.VMEM((NV, 1, COLS), F32),
            pltpu.VMEM((NV, 8, COLS), F32),
            pltpu.VMEM((8, 256), jnp.int32),
            pltpu.VMEM((512, 512), jnp.int32),
            pltpu.VMEM((8, 8, 128), BF16),
            pltpu.VMEM((NZ, 8, 128), BF16),
            pltpu.VMEM((NV, 128, 128), BF16),
            pltpu.VMEM((NY, 8, 64, 128), BF16),
            pltpu.VMEM((NY, 8, 64, 128), BF16),
            pltpu.VMEM((2, NY, 512, 512), BF16),
            pltpu.VMEM((2, 128, 512), F32),
            pltpu.VMEM((2, NY, 8, 512), F32),
            pltpu.VMEM((NV, 144, 128), BF16),
            pltpu.VMEM((NV, 144, 128), BF16),
            pltpu.VMEM((144, 128), BF16),
            pltpu.VMEM((144, 128), BF16),
            pltpu.VMEM((128, 128), BF16),
            pltpu.VMEM((NV, 64, 128), BF16),
            pltpu.VMEM((2, NY, 128, COLS), BF16),
            pltpu.VMEM((8, 8, COLS), BF16),
            pltpu.VMEM((8, 8, COLS), BF16),
            pltpu.VMEM((8, COLS), BF16),
            pltpu.VMEM((2, NX, NY, 4, NC, 8, COLS), BF16),
            pltpu.VMEM((2, ROWS, WIDTH), BF16),
            pltpu.VMEM((256, WIDTH), BF16),
            pltpu.VMEM((256, 128), F32),
            pltpu.VMEM((2, ROWS, 256), F32),
            pltpu.VMEM((8, 8, 128), F32),
            pltpu.VMEM((NZ, 8, 128), F32),
            pltpu.VMEM((8, 128), F32),
            pltpu.VMEM((16, 8, 128), F32),
            dma((8, 2)),
            dma((8, 2)),
            dma((8, NY)),
            dma((8, NY)),
            dma((NY, 8)),
            dma((NY, 8)),
            dma((NZ,)),
            dma((NZ,)),
            dma((NV,)),
            dma((NV,)),
            dma((NV,)),
            dma((NV,)),
            dma((1,)),
            dma((1,)),
            dma((NV,)),
            dma((NV,)),
            dma((NY,)),
            dma((2, NY)),
            dma((NY,)),
            dma((8,)),
            dma((8,)),
            dma((NZ,)),
            dma((8, NC)),
            dma((2, 4)),
            dma((2, 4)),
            dma((2, 4, 2)),
            dma((2, 4, 2)),
            dma((2, 4)),
            dma((2, 4)),
            dma((1,)),
            dma((1,)),
            dma((8,)),
            dma((NZ,)),
            dma((16, NC)),
            dma((16,)),
            dma((9,)),
        ],
        compiler_params=pltpu.CompilerParams(
            collective_id=0, has_side_effects=True, vmem_limit_bytes=60 * 2**20
        ),
        cost_estimate=pl.CostEstimate(
            flops=3_000_000_000, bytes_accessed=8_000_000, transcendentals=2_500_000
        ),
    )(
        span_offset,
        queries,
        cached_keys,
        cached_values,
        out_weight,
        residual,
        norm_gain,
        head_weight,
        targets,
    )
    return out[0, :8]


def solution(mesh):
    return jax.shard_map(
        body,
        mesh=mesh,
        in_specs=(
            P("seq", None),
            P(("seq", "vocab"), None),
            P(("seq", "vocab"), None),
            P("seq", "vocab"),
            P("seq", "vocab"),
            P(),
            P(("seq", "vocab"), None),
            P(),
            P(),
        ),
        out_specs=P("seq"),
        check_vma=False,
    )
```
